512 devices in a mesh: ctx: 64 (over z, y), kv: 8 (over x, core).
Axes of the slice: x: 4, y: 4, z: 16, core: 2. Of those that a mesh axis runs over, the one named last changes fastest.
Arguments:
- cache_keys: bfloat16 [32768, 1024], P('ctx', 'kv'), may hold values from -6 to 6
- cache_values: bfloat16 [32768, 1024], P('ctx', 'kv'), may hold values from -6 to 6
- importance: bfloat16 [8, 32768], P('kv', 'ctx'), may hold values from 0.099609375 to 10
- assignment: int32 [32768], P('ctx'), may hold values from 0 to 32767, as said below
- queries: bfloat16 [128, 8192], P(None, 'kv'), may hold values from -40 to 40
Outputs:
- merged_keys: bfloat16 [32768, 1024], P('ctx', 'kv')
- merged_values: bfloat16 [32768, 1024], P('ctx', 'kv')
- attended: bfloat16 [128, 8192], P(None, 'kv')
The draws below stay inside these ranges and needn't reach their ends.
Inputs may be any that keep to these rules, and one draw needn't show every extreme that they name: `assignment`: each entry is the row itself (the row is kept) or a kept row other than itself (the row is evicted and merges into it). The first row of every aligned block of 128 rows is kept and no row merges into it; in every aligned block between a quarter and five twelfths of the rows, rounded down, are evicted. A shard is an aligned block of 512 rows; shard numbers are taken modulo the number of shards. Of the rows of one shard, at most 16 merge into rows of the shard before it and at most 16 into rows of the shard after it, and into rows of every other shard at least 0 and at most 1. The bounds 16 and 1 are reached in every draw.
All inputs are finite; a program needn't handle non-finite values.
Results may differ from the reference program's by a relative error of at most 0.0055.
Values may be sent and summed in bfloat16 or wider, within the bound.
No kernel may reach another device: no remote copies, remote signals or barrier semaphores. Data moves between devices by JAX's collectives and lax.ppermute only.
A program may use at most 192 MiB of HBM per device.

```python
import math
import jax
import jax.numpy as jnp
from jax import lax

HQ = 64
KVH = 8
HD = 128
ROWS_DEV = 512
BLOCK = 128
NEAR = 16
FAR = 1
GROUP = 8
QTOT = 128
CTX_ROWS = 32768
N_CTX = 64


def key_field(key):
    normal_part = jax.random.normal(jax.random.fold_in(key, 101), (CTX_ROWS, KVH * HD), jnp.float32)
    return normal_part


def draw_cache_keys(key, part):
    field_values = key_field(key)
    return jnp.clip(field_values, -6.0, 6.0).astype(jnp.bfloat16)


def draw_queries(key, part):
    key = jax.random.fold_in(key, 2)
    drawn = jnp.clip(3.5 * jax.random.normal(key, (QTOT, HQ * HD), jnp.float32), -21.0, 21.0)
    return drawn.astype(jnp.bfloat16)


def draw_assignment(key, part):
    key = jax.random.fold_in(key, 3)
    parts_key = jax.random.split(key, 9)
    block_count = ROWS_DEV // BLOCK
    total_rows = N_CTX * ROWS_DEV
    evicted_count = jax.random.randint(parts_key[0], (N_CTX, block_count, 1), BLOCK // 4, BLOCK * 5 // 12 + 1)
    shuffle = jax.random.randint(parts_key[1], (N_CTX, block_count, BLOCK), 0, 1 << 20) * BLOCK + jnp.arange(BLOCK, dtype=jnp.int32)
    shuffle = shuffle.at[:, :, 0].set(jnp.int32(1 << 30))
    slot_order = jnp.argsort(jnp.argsort(shuffle, axis=2), axis=2)
    evicted = (slot_order < evicted_count).reshape(N_CTX, ROWS_DEV)
    row_ids = jnp.arange(ROWS_DEV, dtype=jnp.int32)
    order_key = jnp.where(evicted, jax.random.randint(parts_key[2], (N_CTX, ROWS_DEV), 0, 1 << 18), 1 << 18) * ROWS_DEV + row_ids
    queue_turn = jnp.argsort(jnp.argsort(order_key, axis=1), axis=1)
    shard_ids = jnp.arange(N_CTX, dtype=jnp.int32)
    far_shards = N_CTX - 3
    back_count = jnp.where(shard_ids == jax.random.randint(parts_key[3], (), 0, N_CTX), NEAR, jax.random.randint(parts_key[4], (N_CTX,), NEAR // 4, NEAR + 1))[:, None]
    ahead_count = jnp.where(shard_ids == jax.random.randint(parts_key[5], (), 0, N_CTX), NEAR, jax.random.randint(parts_key[6], (N_CTX,), NEAR // 4, NEAR + 1))[:, None]
    far_count = jax.random.randint(parts_key[7], (N_CTX,), far_shards * (FAR - 1) + 1, far_shards * FAR + 1)[:, None]
    far_turn = queue_turn - back_count - ahead_count
    step_out = jnp.where(queue_turn < back_count, N_CTX - 1, jnp.where(queue_turn < back_count + ahead_count, 1, jnp.where(far_turn < far_count, 2 + far_turn % far_shards, 0)))
    destination = (shard_ids[:, None] + step_out) % N_CTX
    eligible = jnp.logical_and(jnp.logical_not(evicted), (row_ids % BLOCK != 0)[None, :])
    eligible_int = eligible.astype(jnp.int32)
    running = jnp.cumsum(eligible_int.reshape(total_rows))
    per_shard = jnp.sum(eligible_int, axis=1)
    starts = jnp.cumsum(per_shard) - per_shard
    choose = jax.random.randint(parts_key[8], (N_CTX, ROWS_DEV), 0, 1 << 20) % per_shard[destination]
    wanted = starts[destination] + choose + 1
    target = jnp.searchsorted(running, wanted.reshape(total_rows), side='left').astype(jnp.int32)
    return jnp.where(evicted.reshape(total_rows), target, jnp.arange(total_rows, dtype=jnp.int32))


def block_scale(key, shape, shards, smallest, top_value):
    def one(axis_at, parts):
        draws = jax.random.uniform(jax.random.fold_in(jax.random.fold_in(key, 6), axis_at), (parts,), jnp.float32, smallest / len(shards), top_value / len(shards))
        return jnp.repeat(jnp.exp(draws), shape[axis_at] // parts).reshape((-1,) + (1,) * (len(shape) - axis_at - 1))

    factor_of = one(*shards[0])
    for cut in shards[1:]:
        factor_of = factor_of * one(*cut)
    return factor_of


def normal_values(stream_key, extent, width, bound, cuts=(), kind=jnp.bfloat16):
    entries = width * jax.random.normal(stream_key, extent, jnp.float32)
    if cuts:
        entries = entries * block_scale(stream_key, extent, cuts, -0.22, 0.18)
    return jnp.clip(entries, -bound, bound).astype(kind)


def setup_inputs(seed: int = 0) -> dict:
    key_of = jax.random.split(jax.random.key(seed), 6)
    cache_keys = draw_cache_keys(jax.random.fold_in(key_of[5], 71), 0)
    cache_values = normal_values(key_of[1], (CTX_ROWS, KVH * HD), 1.0, 6.0, ((0, 64), (1, 8)))
    importance = jnp.clip(jnp.exp(math.log(10.0) - 4.609084 * jax.random.uniform(key_of[2], (KVH, CTX_ROWS), jnp.float32) ** block_scale(key_of[2], (KVH, CTX_ROWS), ((0, 8), (1, 64)), -0.2, 0.2)), 0.099609375, 10.0).astype(jnp.bfloat16)
    assignment = draw_assignment(jax.random.fold_in(key_of[5], 71), 0)
    queries = draw_queries(jax.random.fold_in(key_of[5], 71), 0)
    return {"cache_keys": cache_keys, "cache_values": cache_values, "importance": importance, "assignment": assignment, "queries": queries}


def merge_field(source_field, row_weight, assignment, kept_rows, denominator):
    widened = source_field.astype(jnp.float32)
    weighted = widened * row_weight.astype(jnp.float32)[:, None]
    numerator = jnp.zeros(source_field.shape, jnp.float32).at[assignment].add(weighted)
    safe_total = jnp.where(kept_rows, denominator, jnp.float32(1.0))
    blended = jnp.where(kept_rows[:, None], numerator / safe_total[:, None], widened)
    return blended.astype(jnp.bfloat16)


def attend_head(query_block, key_rows, value_rows, kept_rows):
    block_count = CTX_ROWS // ROWS_DEV
    key_blocks = key_rows.reshape(block_count, ROWS_DEV, HD)
    value_blocks = value_rows.reshape(block_count, ROWS_DEV, HD)
    live_blocks = kept_rows.reshape(block_count, ROWS_DEV)
    query_rows = query_block.shape[0]

    def advance(running, pieces):
        peak_score, weight_sum, accumulated = running
        key_piece, value_piece, live_piece = pieces
        scores = jnp.dot(query_block, key_piece.astype(jnp.float32).T) * (HD ** -0.5)
        scores = jnp.where(live_piece[None, :], scores, -jnp.inf)
        new_peak = jnp.maximum(peak_score, jnp.max(scores, axis=1))
        weights = jnp.exp(scores - new_peak[:, None])
        rescale = jnp.exp(peak_score - new_peak)
        rounded = lax.optimization_barrier(weights.astype(jnp.bfloat16)).astype(jnp.float32)
        weight_sum = weight_sum * rescale + jnp.sum(weights, axis=1)
        accumulated = accumulated * rescale[:, None] + jnp.dot(rounded, value_piece.astype(jnp.float32))
        return (new_peak, weight_sum, accumulated), None

    start_state = (jnp.full((query_rows,), -jnp.inf, jnp.float32), jnp.zeros((query_rows,), jnp.float32), jnp.zeros((query_rows, HD), jnp.float32))
    final_state, unused_out = lax.scan(advance, start_state, (key_blocks, value_blocks, live_blocks))
    return final_state[2] / final_state[1][:, None]


def reference(cache_keys, cache_values, importance, assignment, queries):
    row_weight = jnp.sum(importance.astype(jnp.float32), axis=0).astype(jnp.bfloat16)
    kept_rows = assignment == jnp.arange(CTX_ROWS, dtype=jnp.int32)
    denominator = jnp.zeros((CTX_ROWS,), jnp.float32).at[assignment].add(row_weight.astype(jnp.float32))
    grouped = queries.astype(jnp.float32).reshape(QTOT, KVH, GROUP, HD)
    key_parts = []
    value_parts = []
    output_parts = []
    for head_index in range(KVH):
        low = head_index * HD
        merged_key = merge_field(cache_keys[:, low:low + HD], row_weight, assignment, kept_rows, denominator)
        merged_value = merge_field(cache_values[:, low:low + HD], row_weight, assignment, kept_rows, denominator)
        key_parts.append(merged_key)
        value_parts.append(merged_value)
        query_block = grouped[:, head_index].reshape(QTOT * GROUP, HD)
        head_output = attend_head(query_block, merged_key, merged_value, kept_rows)
        output_parts.append(head_output.reshape(QTOT, GROUP * HD))
    merged_keys = jnp.concatenate(key_parts, axis=1)
    merged_values = jnp.concatenate(value_parts, axis=1)
    attended = jnp.concatenate(output_parts, axis=1).astype(jnp.bfloat16)
    return (merged_keys, merged_values, attended)
```

```python
import functools

import jax
import jax.numpy as jnp
from jax import lax
from jax.experimental import pallas as pl
from jax.experimental.pallas import tpu as pltpu
from jax.sharding import PartitionSpec as P

NEAR = 16
LANES = 128
PIECES = 4
STATS = 8
F32 = jnp.float32
BF16 = jnp.bfloat16


def summed_weight(importance):
    return jnp.sum(importance.astype(F32), axis=0, keepdims=True).astype(BF16).astype(F32)


def pack_kernel(shards, shard_ref, assignment_ref, importance_ref, keys_ref, values_ref, far_ref, ahead_ref, back_ref):
    row_count = keys_ref.shape[0]
    shard = shard_ref[0]
    assignment = assignment_ref[...]
    owner = assignment // row_count
    target = assignment % row_count
    distance = owner - shard
    distance = jnp.where(distance < 0, distance + shards, distance)
    is_ahead = distance == 1
    is_back = distance == shards - 1
    side = lax.broadcasted_iota(jnp.int32, (8, row_count), 0)
    flags = jnp.where(side == 0, is_ahead.astype(F32), jnp.where(side == 1, is_back.astype(F32), 0.0))
    earlier = lax.broadcasted_iota(jnp.int32, (row_count, row_count), 0) < lax.broadcasted_iota(
        jnp.int32, (row_count, row_count), 1
    )
    ranks = jnp.dot(flags.astype(BF16), earlier.astype(F32).astype(BF16), preferred_element_type=F32)
    ranks = ranks.astype(jnp.int32)
    slot = jnp.where(distance == 0, -1, owner)
    slot = jnp.where(is_ahead, shards + ranks[0:1, :], slot)
    slot = jnp.where(is_back, shards + NEAR + ranks[1:2, :], slot)
    slots = shards + 2 * NEAR
    weight = summed_weight(importance_ref[...])
    part = lax.broadcasted_iota(jnp.int32, (LANES, row_count), 0)
    high = (target // LANES).astype(F32)
    low = (target % LANES).astype(F32)
    notes = jnp.where(part == 0, weight, jnp.where(part == 1, high, jnp.where(part == 2, low, 0.0))).astype(BF16)
    line = lax.broadcasted_iota(jnp.int32, (PIECES * slots, row_count), 0)
    chosen = (line // PIECES == slot).astype(F32).astype(BF16)
    rows = jnp.concatenate([keys_ref[...], values_ref[...]], axis=1)
    picked = jnp.dot(chosen, rows, preferred_element_type=F32)
    noted = lax.dot_general(chosen, notes, (((1,), (1,)), ((), ())), preferred_element_type=F32)
    piece = lax.broadcasted_iota(jnp.int32, (PIECES * slots, LANES), 0) % PIECES
    packed = jnp.where(
        piece == 0,
        picked[:, :LANES],
        jnp.where(piece == 1, picked[:, LANES:], jnp.where(piece == 2, noted, 0.0)),
    ).astype(BF16)
    far = PIECES * shards
    near = PIECES * NEAR
    far_ref[...] = packed[:far]
    ahead_ref[...] = packed[far : far + near]
    back_ref[...] = packed[far + near :]


def split_parts(value, count):
    parts = []
    for _ in range(count):
        rounded = value.astype(BF16).astype(F32)
        parts.append(rounded)
        value = value - rounded
    return parts


def attend_kernel(
    shards,
    shard_ref,
    assignment_ref,
    importance_ref,
    keys_ref,
    values_ref,
    far_ref,
    ahead_ref,
    back_ref,
    queries_ref,
    merged_keys_ref,
    merged_values_ref,
    partial_ref,
):
    row_count, head_dim = keys_ref.shape
    shard = shard_ref[0]
    assignment = assignment_ref[...]
    own = shard * row_count + lax.broadcasted_iota(jnp.int32, (1, row_count), 1)
    kept = assignment == own
    weight = summed_weight(importance_ref[...])
    at_home = assignment // row_count == shard
    target = jnp.where(at_home, assignment % row_count, -1)
    line = lax.broadcasted_iota(jnp.int32, (row_count, row_count), 0)
    home_mix = jnp.where(target == line, weight, 0.0).astype(BF16)
    own_rows = jnp.concatenate([keys_ref[...], values_ref[...]], axis=1)
    ones = jnp.ones((row_count, LANES), BF16)
    sums = jnp.dot(home_mix, own_rows, preferred_element_type=F32)
    total = jnp.dot(home_mix, ones, preferred_element_type=F32)

    arrived = jnp.concatenate([far_ref[...], ahead_ref[...], back_ref[...]], axis=0)
    count = arrived.shape[0]
    notes = arrived.astype(F32).T
    far_weight = notes[0:1, :]
    far_target = notes[1:2, :] * LANES + notes[2:3, :]
    piece = lax.broadcasted_iota(jnp.int32, (1, count), 1) % PIECES
    far_target = jnp.where(piece == 2, far_target, -1.0).astype(jnp.int32)
    line = lax.broadcasted_iota(jnp.int32, (row_count, count), 0)
    mix = jnp.where(far_target == line, far_weight, 0.0)
    value_mix = pltpu.roll(mix, count - 1, 1).astype(BF16)
    key_mix = pltpu.roll(mix, count - 2, 1).astype(BF16)
    total = total + jnp.dot(key_mix, jnp.ones((count, LANES), BF16), preferred_element_type=F32)
    key_sums = sums[:, :head_dim] + jnp.dot(key_mix, arrived, preferred_element_type=F32)
    value_sums = sums[:, head_dim:] + jnp.dot(value_mix, arrived, preferred_element_type=F32)
    has_total = total > 0.0
    safe_total = jnp.where(has_total, total, 1.0)
    merged_keys = jnp.where(has_total, key_sums / safe_total, keys_ref[...].astype(F32)).astype(BF16)
    merged_values = jnp.where(has_total, value_sums / safe_total, values_ref[...].astype(F32)).astype(BF16)
    merged_keys_ref[...] = merged_keys
    merged_values_ref[...] = merged_values

    query_rows = queries_ref.shape[0]
    heads = queries_ref.shape[1] // head_dim
    per_peer = query_rows * heads // shards
    peers_of_head = query_rows // per_peer
    scale = head_dim ** (-0.5)
    lane = lax.broadcasted_iota(jnp.int32, (query_rows, LANES), 1)
    peaks = jnp.zeros((query_rows, LANES), F32)
    sizes = jnp.zeros((query_rows, LANES), F32)
    for head in range(heads):
        query = queries_ref[:, head * head_dim : (head + 1) * head_dim]
        scores = lax.dot_general(query, merged_keys, (((1,), (1,)), ((), ())), preferred_element_type=F32)
        scores = jnp.where(kept, scores * scale, -jnp.inf)
        peak = jnp.max(scores, axis=1, keepdims=True)
        prob = jnp.exp(scores - peak)
        size = jnp.sum(prob, axis=1, keepdims=True)
        sums = jnp.dot(prob.astype(BF16), merged_values, preferred_element_type=F32).astype(BF16)
        peaks = jnp.where(lane == head, peak, peaks)
        sizes = jnp.where(lane == head, size, sizes)
        for part in range(peers_of_head):
            partial_ref[head * peers_of_head + part, 0:per_peer, :] = sums[part * per_peer : (part + 1) * per_peer]
    peak_parts = split_parts(peaks.T, 3)
    size_parts = split_parts(sizes.T, 2)
    stat = lax.broadcasted_iota(jnp.int32, (STATS, query_rows), 0)
    for head in range(heads):
        block = jnp.zeros((STATS, query_rows), F32)
        for at, member in enumerate(peak_parts + size_parts):
            block = jnp.where(stat == at, member[head : head + 1, :], block)
        for part in range(peers_of_head):
            partial_ref[head * peers_of_head + part, per_peer : per_peer + STATS, :] = block.astype(BF16)


def combine_kernel(shards, shard_ref, partial_ref, finished_ref, factor_ref):
    per_peer = partial_ref.shape[1] - STATS
    query_rows = partial_ref.shape[2]
    stats = partial_ref[:, per_peer:, :].astype(F32)
    peak = stats[:, 0, :] + stats[:, 1, :] + stats[:, 2, :]
    size = stats[:, 3, :] + stats[:, 4, :]
    rescale = jnp.exp(peak - jnp.max(peak, axis=0, keepdims=True))
    factor = rescale / jnp.sum(rescale * size, axis=0, keepdims=True)
    if shards < LANES:
        factor = jnp.concatenate([factor, jnp.zeros((LANES - shards, query_rows), F32)], axis=0)
    factor_ref[...] = factor.T
    start = pl.multiple_of((shard_ref[0] % (query_rows // per_peer)) * per_peer, per_peer)
    factor = factor_ref[pl.ds(start, per_peer), :]
    total = jnp.zeros((per_peer, LANES), F32)
    for peer in range(shards):
        total = total + factor[:, peer : peer + 1] * partial_ref[peer, 0:per_peer, :].astype(F32)
    finished = total.astype(BF16)
    for peer in range(shards):
        finished_ref[peer] = finished


def in_vmem(count):
    return [pl.BlockSpec(memory_space=pltpu.SMEM)] + [pl.BlockSpec(memory_space=pltpu.VMEM)] * count


def run_kernel(body, shards, shapes, operands, scratch=()):
    return pl.pallas_call(
        functools.partial(body, shards),
        out_shape=[jax.ShapeDtypeStruct(shape, BF16) for shape in shapes],
        in_specs=in_vmem(len(operands) - 1),
        out_specs=[pl.BlockSpec(memory_space=pltpu.VMEM)] * len(shapes),
        scratch_shapes=list(scratch),
        compiler_params=pltpu.CompilerParams(vmem_limit_bytes=32 * 1024 * 1024),
    )(*operands)


def per_device(cache_keys, cache_values, importance, assignment, queries):
    row_count, head_dim = cache_keys.shape
    query_rows = queries.shape[0]
    heads = queries.shape[1] // head_dim
    shards = lax.axis_size("ctx")
    per_peer = query_rows * heads // shards
    shard = lax.axis_index("ctx").astype(jnp.int32).reshape(1)
    assignment = assignment.reshape(1, row_count)
    importance = lax.all_gather(importance, "kv", axis=0, tiled=True)

    far, ahead, back = run_kernel(
        pack_kernel,
        shards,
        [(PIECES * shards, LANES), (PIECES * NEAR, LANES), (PIECES * NEAR, LANES)],
        (shard, assignment, importance, cache_keys, cache_values),
    )
    from_back = lax.ppermute(ahead, "ctx", [(i, (i + 1) % shards) for i in range(shards)])
    from_ahead = lax.ppermute(back, "ctx", [(i, (i - 1) % shards) for i in range(shards)])
    far = lax.all_to_all(far.reshape(shards, PIECES, LANES), "ctx", 0, 0, tiled=True)
    far = far.reshape(shards * PIECES, LANES)

    merged_keys, merged_values, partial = run_kernel(
        attend_kernel,
        shards,
        [cache_keys.shape, cache_values.shape, (shards, per_peer + STATS, LANES)],
        (shard, assignment, importance, cache_keys, cache_values, far, from_back, from_ahead, queries),
    )
    partial = lax.all_to_all(partial, "ctx", 0, 0, tiled=True)
    (finished,) = run_kernel(
        combine_kernel,
        shards,
        [(shards, per_peer, LANES)],
        (shard, partial),
        [pltpu.VMEM((query_rows, LANES), F32)],
    )
    finished = lax.all_to_all(finished, "ctx", 0, 0, tiled=True)
    attended = finished.reshape(heads, query_rows, head_dim).transpose(1, 0, 2).reshape(query_rows, heads * head_dim)
    return (merged_keys, merged_values, attended)


def solution(mesh):
    placed = (P("ctx", "kv"), P("ctx", "kv"), P("kv", "ctx"), P("ctx"), P(None, "kv"))
    return jax.shard_map(
        per_device,
        mesh=mesh,
        in_specs=placed,
        out_specs=(P("ctx", "kv"), P("ctx", "kv"), P(None, "kv")),
        check_vma=False,
    )
```

```python
import functools

import jax
import jax.numpy as jnp
from jax import lax
from jax.experimental import pallas as pl
from jax.experimental.pallas import tpu as pltpu
from jax.sharding import PartitionSpec as P

NEAR = 16
LANES = 128
TILE = 8
PIECES = 4
NOTES = 2
PEAK_PARTS = 3
SIZE_PARTS = 2
F32 = jnp.float32
BF16 = jnp.bfloat16


def rows_of(shape):
    return lax.broadcasted_iota(jnp.int32, shape, 0)


def lanes_of(shape):
    return lax.broadcasted_iota(jnp.int32, shape, 1)


def onehot(flags):
    return flags.astype(F32).astype(BF16)


def row_weight(importance):
    summed = jnp.sum(importance.astype(F32), axis=0).astype(BF16).astype(F32)
    return jnp.concatenate([summed[at : at + 1, :] for at in range(summed.shape[0])], axis=1)


def split_parts(value, count):
    parts = []
    for _ in range(count):
        rounded = value.astype(BF16).astype(F32)
        parts.append(rounded)
        value = value - rounded
    return parts


def peer_place(index, span):
    peer = index // span
    return peer, index - peer * span


def pull(sources, targets, semaphore):
    copies = [
        pltpu.make_async_copy(source, target, semaphore.at[at])
        for at, (source, target) in enumerate(zip(sources, targets))
    ]
    for copy in copies:
        copy.start()
    for copy in copies:
        copy.wait()


def destination(shards, shard, assignment, row_count):
    owner = assignment // row_count
    distance = owner - shard
    distance = jnp.where(distance < 0, distance + shards, distance)
    ahead = distance == 1
    back = distance == shards - 1
    side = rows_of((TILE, row_count))
    flags = jnp.where(side == 0, ahead.astype(F32), jnp.where(side == 1, back.astype(F32), 0.0)).astype(BF16)
    earlier = onehot(rows_of((row_count, row_count)) < lanes_of((row_count, row_count)))
    ranks = jnp.dot(flags, earlier, preferred_element_type=F32).astype(jnp.int32)
    rank = jnp.where(ahead, ranks[0:1, :], jnp.where(back, ranks[1:2, :], 0))
    peer = jnp.where(distance == 0, -1, owner)
    far_peer = jnp.where(ahead | back, -1, peer)
    return peer, far_peer, ahead, back, rank


def chosen_rows(shards, peer, far_peer, row_count):
    line = rows_of((PIECES * shards, row_count))
    return onehot(line // PIECES == jnp.where(line % PIECES == NOTES, peer, far_peer))


def rows_kernel(
    shards, shard_ref, assignment_hbm, keys_hbm, values_hbm, far_ref, ahead_ref, back_ref, peer_ref,
    assignment_ref, keys_ref, values_ref, semaphore,
):
    pull((assignment_hbm, keys_hbm, values_hbm), (assignment_ref, keys_ref, values_ref), semaphore)
    row_count = keys_ref.shape[0]
    assignment = assignment_ref[...]
    peer, far_peer, ahead, back, rank = destination(shards, shard_ref[0], assignment, row_count)
    rows = jnp.concatenate([keys_ref[...], values_ref[...]], axis=1)
    slot = jnp.where(ahead, rank, jnp.where(back, NEAR + rank, -1))
    near = jnp.dot(onehot(rows_of((2 * NEAR, row_count)) == slot), rows, preferred_element_type=F32).astype(BF16)
    ahead_ref[...] = jnp.concatenate([near[:NEAR, :LANES], near[:NEAR, LANES:]], axis=0)
    back_ref[...] = jnp.concatenate([near[NEAR:, :LANES], near[NEAR:, LANES:]], axis=0)
    chosen = chosen_rows(shards, peer, far_peer, row_count)
    picked = jnp.dot(chosen, rows, preferred_element_type=F32)
    target = assignment % row_count
    part = rows_of((LANES, row_count))
    place = jnp.where(
        part // NEAR == 1, (target // LANES).astype(F32), jnp.where(part // NEAR == 2, (target % LANES).astype(F32), 0.0)
    )
    notes = jnp.where(part % NEAR == rank, place, 0.0).astype(BF16)
    noted = lax.dot_general(chosen, notes, (((1,), (1,)), ((), ())), preferred_element_type=F32)
    piece = rows_of((PIECES * shards, LANES)) % PIECES
    far_ref[...] = jnp.where(
        piece == 0, picked[:, :LANES], jnp.where(piece == 1, picked[:, LANES:], jnp.where(piece == NOTES, noted, 0.0))
    ).astype(BF16)
    at = rows_of((TILE, row_count))
    peer_ref[...] = jnp.where(at == 0, peer, jnp.where(at == 1, far_peer, rank))


def weigh_kernel(shards, importance_ref, peer_ref, far_ref, out_ref):
    row_count = peer_ref.shape[1]
    weight = row_weight(importance_ref[...])
    peer, far_peer, rank = peer_ref[0:1, :], peer_ref[1:2, :], peer_ref[2:3, :]
    chosen = chosen_rows(shards, peer, far_peer, row_count)
    notes = jnp.where(rows_of((LANES, row_count)) == rank, weight, 0.0).astype(BF16)
    noted = lax.dot_general(chosen, notes, (((1,), (1,)), ((), ())), preferred_element_type=F32)
    piece = rows_of((PIECES * shards, LANES)) % PIECES
    out_ref[...] = (far_ref[...].astype(F32) + jnp.where(piece == NOTES, noted, 0.0)).astype(BF16)


def home_kernel(
    shards, shard_ref, importance_ref, assignment_hbm, keys_hbm, values_hbm, queries_hbm,
    sums_ref, total_ref, bias_ref, padded_ref, assignment_ref, keys_ref, values_ref, queries_ref, semaphore,
):
    pull(
        (assignment_hbm, keys_hbm, values_hbm, queries_hbm),
        (assignment_ref, keys_ref, values_ref, queries_ref),
        semaphore,
    )
    row_count, head_dim = keys_ref.shape
    shard = shard_ref[0]
    assignment = assignment_ref[...]
    weight = row_weight(importance_ref[...])
    target = jnp.where(assignment // row_count == shard, assignment % row_count, -1)
    index = lanes_of((1, row_count))
    kept = target == index
    line = rows_of((row_count, row_count))
    mix = jnp.where(target == line, weight, jnp.where((index == line) & jnp.logical_not(kept), 1.0, 0.0)).astype(BF16)
    rows = jnp.concatenate([keys_ref[...], values_ref[...]], axis=1)
    sums_ref[...] = jnp.dot(mix, rows, preferred_element_type=F32)
    total_ref[...] = jnp.dot(mix, jnp.ones((row_count, LANES), BF16), preferred_element_type=F32)
    bias_ref[...] = jnp.broadcast_to(jnp.where(kept, 0.0, -jnp.inf), bias_ref.shape)

    query_rows = queries_ref.shape[0]
    heads = queries_ref.shape[1] // head_dim
    per_peer = query_rows * heads // shards
    span = per_peer + 2
    group = per_peer * heads
    peers = group // per_peer
    peer, place = peer_place(rows_of((peers * span, group)), span)
    per_tile = heads * TILE // per_peer
    head = (peer % per_tile) * (per_peer // TILE) + place // TILE
    source = head * per_peer + (peer // per_tile) * TILE + place % TILE
    order = onehot((source == lanes_of((peers * span, group))) & (place < per_peer))
    for part in range(query_rows // per_peer):
        block = queries_ref[part * per_peer : (part + 1) * per_peer, :]
        block = jnp.concatenate([block[:, at * head_dim : (at + 1) * head_dim] for at in range(heads)], axis=0)
        moved = jnp.dot(order, block, preferred_element_type=F32).astype(BF16)
        padded_ref[part * peers * span : (part + 1) * peers * span, :] = moved


def attend_kernel(
    shards, shard_ref, sums_ref, total_ref, bias_ref, padded_ref, far_ref, from_back_ref, from_ahead_ref,
    merged_ref, partial_ref,
):
    row_count = sums_ref.shape[0]
    shard = shard_ref[0]
    back = jnp.where(shard == 0, shards - 1, shard - 1)
    ahead = jnp.where(shard == shards - 1, 0, shard + 1)
    far = far_ref[...]
    count = far.shape[0]
    notes = far.astype(F32).T
    lane = lanes_of((1, count))
    source = lane // PIECES
    is_far = (lane % PIECES == NOTES) & (source != back) & (source != ahead) & (source != shard)
    far_weight = notes[0:1, :]
    far_target = jnp.where(is_far, notes[NEAR : NEAR + 1, :] * LANES + notes[2 * NEAR : 2 * NEAR + 1, :], -1.0)

    line = rows_of((TILE, count))
    wanted = jnp.where(line == 0, back, ahead) * PIECES + NOTES
    picked = onehot((lanes_of((TILE, count)) == wanted) & (line < 2))
    near_notes = jnp.dot(picked, far, preferred_element_type=F32)
    near_target = (
        pltpu.roll(near_notes, LANES - NEAR, 1) * LANES + pltpu.roll(near_notes, LANES - 2 * NEAR, 1)
    )
    lane = lanes_of((1, LANES))
    second = (lane >= 2 * NEAR) & (lane < 3 * NEAR)
    shifted_notes = pltpu.roll(near_notes, 2 * NEAR, 1)
    shifted_target = pltpu.roll(near_target, 2 * NEAR, 1)
    near_weight = jnp.where(lane < NEAR, near_notes[0:1, :], shifted_notes[1:2, :])
    near_place = jnp.where(lane < NEAR, near_target[0:1, :], jnp.where(second, shifted_target[1:2, :], -1.0))

    line = rows_of((row_count, count + LANES))

    def mixing(far_shift, near_shift):
        def moved(value, shift):
            value = jnp.broadcast_to(value, (TILE, value.shape[1]))
            return pltpu.roll(value, shift, 1)[0:1, :] if shift else value[0:1, :]

        target = jnp.concatenate([moved(far_target, far_shift), moved(near_place, near_shift)], axis=1)
        weight = jnp.concatenate([moved(far_weight, far_shift), moved(near_weight, near_shift)], axis=1)
        return jnp.where(target.astype(jnp.int32) == line, weight, 0.0).astype(BF16)

    key_mix = mixing(count - NOTES, 0)
    value_mix = mixing(count - NOTES + 1, NEAR)
    arrived = jnp.concatenate(
        [far, from_back_ref[...], from_ahead_ref[...], jnp.zeros((LANES - 4 * NEAR, LANES), BF16)], axis=0
    )
    total = total_ref[...] + jnp.dot(key_mix, jnp.ones(arrived.shape, BF16), preferred_element_type=F32)
    merged_keys = (sums_ref[:, :LANES] + jnp.dot(key_mix, arrived, preferred_element_type=F32)) / total
    merged_values = (sums_ref[:, LANES:] + jnp.dot(value_mix, arrived, preferred_element_type=F32)) / total
    merged_keys = merged_keys.astype(BF16)
    merged_values = merged_values.astype(BF16)
    merged_ref[0] = merged_keys
    merged_ref[1] = merged_values

    span = padded_ref.shape[0] // shards
    per_peer = span - 2
    scale = LANES ** (-0.5)
    bias = bias_ref[0:1, :]
    group = TILE * span
    peer, place = peer_place(rows_of((group, LANES)), span)
    lane = lanes_of((group, LANES))
    part = lane // per_peer
    diagonal = place == lane % per_peer
    from_peer, from_place = peer_place(lanes_of((group, group)), span)
    to_peer, to_place = peer_place(rows_of((group, group)), span)
    gather = onehot((to_place == per_peer) & (from_peer == to_peer) & (from_place < per_peer))
    for at in range(0, padded_ref.shape[0], group):
        scores = lax.dot_general(
            padded_ref[at : at + group, :], merged_keys, (((1,), (1,)), ((), ())), preferred_element_type=F32
        )
        scores = scores * scale + bias
        peak = jnp.max(scores, axis=1, keepdims=True)
        prob = jnp.exp(scores - peak)
        size = jnp.sum(prob, axis=1, keepdims=True)
        sums = jnp.dot(prob.astype(BF16), merged_values, preferred_element_type=F32)
        stats = jnp.zeros((group, LANES), F32)
        for which, member in enumerate(split_parts(peak, PEAK_PARTS) + split_parts(size, SIZE_PARTS)):
            stats = jnp.where(part == which, member, stats)
        stats = jnp.where(diagonal, stats, 0.0).astype(BF16)
        stats = jnp.dot(gather, stats, preferred_element_type=F32)
        partial_ref[at : at + group, :] = jnp.where(place < per_peer, sums, stats).astype(BF16)


def combine_kernel(shards, partial_ref, finished_ref):
    count = partial_ref.shape[0]
    span = count // shards
    per_peer = span - 2
    partial = partial_ref[...]
    wide = (shards, count)
    picked = onehot(lanes_of(wide) == rows_of(wide) * span + per_peer)
    stats = jnp.dot(picked, partial, preferred_element_type=F32)

    def part(which):
        return pltpu.roll(stats, LANES - which * per_peer, 1) if which else stats

    valid = lanes_of((shards, LANES)) < per_peer
    peak = jnp.where(valid, (part(0) + part(1)) + part(2), 0.0)
    size = jnp.where(valid, part(3) + part(4), 1.0)
    rescale = jnp.exp(peak - jnp.max(peak, axis=0, keepdims=True))
    factor = rescale / jnp.sum(rescale * size, axis=0, keepdims=True)
    factor = jnp.concatenate([factor, jnp.zeros((LANES - shards, LANES), F32)], axis=0).T[:per_peer, :shards]
    factor = jnp.concatenate(split_parts(factor, 2), axis=0).astype(BF16)
    start = rows_of(wide) * span
    spread = onehot((lanes_of(wide) >= start) & (lanes_of(wide) < start + span))
    factor = jnp.dot(factor, spread, preferred_element_type=F32)
    unused, place = peer_place(lanes_of(factor.shape), span)
    factor = jnp.where(place == rows_of(factor.shape) % per_peer, factor, 0.0).astype(BF16)
    total = jnp.dot(factor, partial, preferred_element_type=F32)
    finished = (total[:per_peer] + total[per_peer:]).astype(BF16)
    for peer in range(shards):
        finished_ref[peer] = finished


SMEM = pl.BlockSpec(memory_space=pltpu.SMEM)
VMEM = pl.BlockSpec(memory_space=pltpu.VMEM)
ANY = pl.BlockSpec(memory_space=pl.ANY)


def run_kernel(body, shards, shapes, specs, operands, pulled=()):
    scratch = [pltpu.VMEM(member.shape, member.dtype) for member in pulled]
    if pulled:
        scratch.append(pltpu.SemaphoreType.DMA((len(pulled),)))
    return pl.pallas_call(
        functools.partial(body, shards),
        out_shape=[jax.ShapeDtypeStruct(shape, dtype) for shape, dtype in shapes],
        in_specs=specs,
        out_specs=[VMEM] * len(shapes),
        scratch_shapes=scratch,
        compiler_params=pltpu.CompilerParams(vmem_limit_bytes=24 * 1024 * 1024),
    )(*operands)


def per_device(cache_keys, cache_values, importance, assignment, queries):
    row_count, head_dim = cache_keys.shape
    query_rows = queries.shape[0]
    heads = queries.shape[1] // head_dim
    shards = lax.axis_size("ctx")
    groups = lax.axis_size("kv")
    per_peer = query_rows * heads // shards
    span = per_peer + 2
    shard = lax.axis_index("ctx").astype(jnp.int32).reshape(1)
    assignment = assignment.reshape(1, row_count)

    copies = jnp.broadcast_to(importance.reshape(1, row_count // LANES, LANES), (groups, row_count // LANES, LANES))
    importance = lax.all_to_all(copies, "kv", 0, 0, tiled=True)
    pulled = (assignment, cache_keys, cache_values)
    far, ahead, back, peer = run_kernel(
        rows_kernel,
        shards,
        [
            ((PIECES * shards, LANES), BF16),
            ((2 * NEAR, LANES), BF16),
            ((2 * NEAR, LANES), BF16),
            ((TILE, row_count), jnp.int32),
        ],
        [SMEM, ANY, ANY, ANY],
        (shard,) + pulled,
        pulled,
    )
    from_back = lax.ppermute(ahead, "ctx", [(i, (i + 1) % shards) for i in range(shards)])
    from_ahead = lax.ppermute(back, "ctx", [(i, (i - 1) % shards) for i in range(shards)])
    (far,) = run_kernel(
        weigh_kernel, shards, [((PIECES * shards, LANES), BF16)], [VMEM, VMEM, VMEM], (importance, peer, far)
    )
    far, importance = lax.optimization_barrier((far, importance))
    far = lax.all_to_all(far.reshape(shards, PIECES, LANES), "ctx", 0, 0, tiled=True)
    pulled = (assignment, cache_keys, cache_values, queries)
    sums, total, bias, padded = run_kernel(
        home_kernel,
        shards,
        [
            ((row_count, 2 * head_dim), F32),
            ((row_count, LANES), F32),
            ((TILE, row_count), F32),
            ((shards * span, head_dim), BF16),
        ],
        [SMEM, VMEM, ANY, ANY, ANY, ANY],
        (shard, importance) + pulled,
        pulled,
    )
    merged, partial = run_kernel(
        attend_kernel,
        shards,
        [((2, row_count, head_dim), BF16), ((shards * span, LANES), BF16)],
        [SMEM] + [VMEM] * 7,
        (shard, sums, total, bias, padded, far.reshape(shards * PIECES, LANES), from_back, from_ahead),
    )
    partial = lax.all_to_all(partial.reshape(shards, span // 2, 2, LANES), "ctx", 0, 0, tiled=True)
    merged_keys = merged[0]
    (finished,) = run_kernel(
        combine_kernel, shards, [((shards, per_peer, LANES), BF16)], [VMEM], (partial.reshape(shards * span, LANES),)
    )
    finished, merged = lax.optimization_barrier((finished, merged))
    finished = lax.all_to_all(finished, "ctx", 0, 0, tiled=True)
    merged_values = merged[1]
    tiles = query_rows // TILE
    attended = finished.reshape(tiles, heads, TILE, head_dim).transpose(0, 2, 1, 3)
    return (merged_keys, merged_values, attended.reshape(query_rows, heads * head_dim))


def solution(mesh):
    placed = (P("ctx", "kv"), P("ctx", "kv"), P("kv", "ctx"), P("ctx"), P(None, "kv"))
    return jax.shard_map(
        per_device,
        mesh=mesh,
        in_specs=placed,
        out_specs=(P("ctx", "kv"), P("ctx", "kv"), P(None, "kv")),
        check_vma=False,
    )
```

```python
import functools

import jax
import jax.numpy as jnp
from jax import lax
from jax.experimental import pallas as pl
from jax.experimental.pallas import tpu as pltpu
from jax.sharding import PartitionSpec as P

NEAR = 16
LANES = 128
TILE = 8
PIECES = 4
NOTES = 2
PEAK_PARTS = 3
SIZE_PARTS = 2
F32 = jnp.float32
BF16 = jnp.bfloat16


def rows_of(shape):
    return lax.broadcasted_iota(jnp.int32, shape, 0)


def lanes_of(shape):
    return lax.broadcasted_iota(jnp.int32, shape, 1)


def onehot(flags):
    return flags.astype(F32).astype(BF16)


def row_weight(importance):
    summed = jnp.sum(importance.astype(F32), axis=0).astype(BF16).astype(F32)
    return jnp.concatenate([summed[at : at + 1, :] for at in range(summed.shape[0])], axis=1)


def split_parts(value, count):
    parts = []
    for _ in range(count):
        rounded = value.astype(BF16).astype(F32)
        parts.append(rounded)
        value = value - rounded
    return parts


def divided(index, size):
    if size & (size - 1):
        return (index * (-(-(1 << 16) // size))) >> 16
    return index >> (size.bit_length() - 1)


def remainder(index, size):
    if size & (size - 1):
        return index - divided(index, size) * size
    return index & (size - 1)


def peer_place(index, span):
    return divided(index, span), remainder(index, span)


def pull(sources, targets, semaphore):
    copies = [
        pltpu.make_async_copy(source, target, semaphore.at[at])
        for at, (source, target) in enumerate(zip(sources, targets))
    ]
    for copy in copies:
        copy.start()
    for copy in copies:
        copy.wait()


def destination(shards, shard, assignment, row_count):
    owner = divided(assignment, row_count)
    distance = owner - shard
    distance = jnp.where(distance < 0, distance + shards, distance)
    ahead = distance == 1
    back = distance == shards - 1
    side = rows_of((TILE, row_count))
    flags = jnp.where(side == 0, ahead.astype(F32), jnp.where(side == 1, back.astype(F32), 0.0)).astype(BF16)
    earlier = onehot(rows_of((row_count, row_count)) < lanes_of((row_count, row_count)))
    ranks = jnp.dot(flags, earlier, preferred_element_type=F32).astype(jnp.int32)
    rank = jnp.where(ahead, ranks[0:1, :], jnp.where(back, ranks[1:2, :], 0))
    peer = jnp.where(distance == 0, -1, owner)
    far_peer = jnp.where(ahead | back, -1, peer)
    return peer, far_peer, ahead, back, rank


def chosen_rows(shards, peer, far_peer, row_count):
    line = rows_of((PIECES * shards, row_count))
    return onehot(divided(line, PIECES) == jnp.where(remainder(line, PIECES) == NOTES, peer, far_peer))


def copy_kernel(shards, importance_ref, copies_ref):
    importance = importance_ref[...].astype(F32)
    slices = importance.shape[1] // LANES
    place = remainder(rows_of(copies_ref.shape), slices)
    copies = jnp.zeros(copies_ref.shape, F32)
    for at in range(slices):
        copies = jnp.where(place == at, importance[:, at * LANES : (at + 1) * LANES], copies)
    copies_ref[...] = copies.astype(BF16)


def rows_kernel(
    shards, shard_ref, assignment_hbm, keys_hbm, values_hbm, far_ref, ahead_ref, back_ref, peer_ref,
    assignment_ref, keys_ref, values_ref, semaphore,
):
    pull((assignment_hbm, keys_hbm, values_hbm), (assignment_ref, keys_ref, values_ref), semaphore)
    row_count = keys_ref.shape[0]
    assignment = assignment_ref[...]
    peer, far_peer, ahead, back, rank = destination(shards, shard_ref[0], assignment, row_count)
    rows = jnp.concatenate([keys_ref[...], values_ref[...]], axis=1)
    slot = jnp.where(ahead, rank, jnp.where(back, NEAR + rank, -1))
    near = jnp.dot(onehot(rows_of((2 * NEAR, row_count)) == slot), rows, preferred_element_type=F32).astype(BF16)
    ahead_ref[...] = jnp.concatenate([near[:NEAR, :LANES], near[:NEAR, LANES:]], axis=0)
    back_ref[...] = jnp.concatenate([near[NEAR:, :LANES], near[NEAR:, LANES:]], axis=0)
    chosen = chosen_rows(shards, peer, far_peer, row_count)
    picked = jnp.dot(chosen, rows, preferred_element_type=F32)
    target = remainder(assignment, row_count)
    part = rows_of((LANES, row_count))
    place = jnp.where(
        divided(part, NEAR) == 1,
        divided(target, LANES).astype(F32),
        jnp.where(divided(part, NEAR) == 2, remainder(target, LANES).astype(F32), 0.0),
    )
    notes = jnp.where(remainder(part, NEAR) == rank, place, 0.0).astype(BF16)
    noted = lax.dot_general(chosen, notes, (((1,), (1,)), ((), ())), preferred_element_type=F32)
    piece = remainder(rows_of((PIECES * shards, LANES)), PIECES)
    far_ref[...] = jnp.where(
        piece == 0, picked[:, :LANES], jnp.where(piece == 1, picked[:, LANES:], jnp.where(piece == NOTES, noted, 0.0))
    ).astype(BF16)
    at = rows_of((TILE, row_count))
    peer_ref[...] = jnp.where(at == 0, peer, jnp.where(at == 1, far_peer, rank))


def weigh_kernel(shards, importance_ref, peer_ref, far_ref, out_ref):
    row_count = peer_ref.shape[1]
    weight = row_weight(importance_ref[...])
    peer, far_peer, rank = peer_ref[0:1, :], peer_ref[1:2, :], peer_ref[2:3, :]
    chosen = chosen_rows(shards, peer, far_peer, row_count)
    notes = jnp.where(rows_of((LANES, row_count)) == rank, weight, 0.0).astype(BF16)
    noted = lax.dot_general(chosen, notes, (((1,), (1,)), ((), ())), preferred_element_type=F32)
    piece = remainder(rows_of((PIECES * shards, LANES)), PIECES)
    out_ref[...] = (far_ref[...].astype(F32) + jnp.where(piece == NOTES, noted, 0.0)).astype(BF16)


def home_kernel(
    shards, shard_ref, importance_ref, assignment_hbm, keys_hbm, values_hbm, queries_hbm,
    sums_ref, total_ref, bias_ref, padded_ref, assignment_ref, keys_ref, values_ref, queries_ref, semaphore,
):
    pull(
        (assignment_hbm, keys_hbm, values_hbm, queries_hbm),
        (assignment_ref, keys_ref, values_ref, queries_ref),
        semaphore,
    )
    row_count, head_dim = keys_ref.shape
    shard = shard_ref[0]
    assignment = assignment_ref[...]
    weight = row_weight(importance_ref[...])
    target = jnp.where(divided(assignment, row_count) == shard, remainder(assignment, row_count), -1)
    index = lanes_of((1, row_count))
    kept = target == index
    line = rows_of((row_count, row_count))
    mix = jnp.where(target == line, weight, jnp.where((index == line) & jnp.logical_not(kept), 1.0, 0.0)).astype(BF16)
    rows = jnp.concatenate([keys_ref[...], values_ref[...]], axis=1)
    sums_ref[...] = jnp.dot(mix, rows, preferred_element_type=F32)
    total_ref[...] = jnp.dot(mix, jnp.ones((row_count, LANES), BF16), preferred_element_type=F32)
    bias_ref[...] = jnp.broadcast_to(jnp.where(kept, 0.0, -jnp.inf), bias_ref.shape)

    query_rows = queries_ref.shape[0]
    heads = queries_ref.shape[1] // head_dim
    per_peer = query_rows * heads // shards
    span = per_peer + 2
    group = per_peer * heads
    peers = group // per_peer
    peer, place = peer_place(rows_of((peers * span, group)), span)
    per_tile = heads * TILE // per_peer
    head = remainder(peer, per_tile) * (per_peer // TILE) + divided(place, TILE)
    source = head * per_peer + divided(peer, per_tile) * TILE + remainder(place, TILE)
    order = onehot((source == lanes_of((peers * span, group))) & (place < per_peer))
    for part in range(query_rows // per_peer):
        block = queries_ref[part * per_peer : (part + 1) * per_peer, :]
        block = jnp.concatenate([block[:, at * head_dim : (at + 1) * head_dim] for at in range(heads)], axis=0)
        moved = jnp.dot(order, block, preferred_element_type=F32).astype(BF16)
        padded_ref[part * peers * span : (part + 1) * peers * span, :] = moved


def attend_kernel(
    shards, shard_ref, sums_ref, total_ref, bias_ref, padded_ref, far_ref, from_back_ref, from_ahead_ref,
    merged_ref, partial_ref,
):
    row_count = sums_ref.shape[0]
    shard = shard_ref[0]
    back = jnp.where(shard == 0, shards - 1, shard - 1)
    ahead = jnp.where(shard == shards - 1, 0, shard + 1)
    far = far_ref[...]
    count = far.shape[0]
    notes = far.astype(F32).T
    lane = lanes_of((1, count))
    source = divided(lane, PIECES)
    is_far = (remainder(lane, PIECES) == NOTES) & (source != back) & (source != ahead) & (source != shard)
    far_weight = notes[0:1, :]
    far_target = jnp.where(is_far, notes[NEAR : NEAR + 1, :] * LANES + notes[2 * NEAR : 2 * NEAR + 1, :], -1.0)

    line = rows_of((TILE, count))
    wanted = jnp.where(line == 0, back, ahead) * PIECES + NOTES
    picked = onehot((lanes_of((TILE, count)) == wanted) & (line < 2))
    near_notes = jnp.dot(picked, far, preferred_element_type=F32)
    near_target = (
        pltpu.roll(near_notes, LANES - NEAR, 1) * LANES + pltpu.roll(near_notes, LANES - 2 * NEAR, 1)
    )
    lane = lanes_of((1, LANES))
    second = (lane >= 2 * NEAR) & (lane < 3 * NEAR)
    shifted_notes = pltpu.roll(near_notes, 2 * NEAR, 1)
    shifted_target = pltpu.roll(near_target, 2 * NEAR, 1)
    near_weight = jnp.where(lane < NEAR, near_notes[0:1, :], shifted_notes[1:2, :])
    near_place = jnp.where(lane < NEAR, near_target[0:1, :], jnp.where(second, shifted_target[1:2, :], -1.0))

    line = rows_of((row_count, count + LANES))

    def mixing(far_shift, near_shift):
        def moved(value, shift):
            value = jnp.broadcast_to(value, (TILE, value.shape[1]))
            return pltpu.roll(value, shift, 1)[0:1, :] if shift else value[0:1, :]

        target = jnp.concatenate([moved(far_target, far_shift), moved(near_place, near_shift)], axis=1)
        weight = jnp.concatenate([moved(far_weight, far_shift), moved(near_weight, near_shift)], axis=1)
        return jnp.where(target.astype(jnp.int32) == line, weight, 0.0).astype(BF16)

    key_mix = mixing(count - NOTES, 0)
    value_mix = mixing(count - NOTES + 1, NEAR)
    arrived = jnp.concatenate(
        [far, from_back_ref[...], from_ahead_ref[...], jnp.zeros((LANES - 4 * NEAR, LANES), BF16)], axis=0
    )
    total = total_ref[...] + jnp.dot(key_mix, jnp.ones(arrived.shape, BF16), preferred_element_type=F32)
    merged_keys = (sums_ref[:, :LANES] + jnp.dot(key_mix, arrived, preferred_element_type=F32)) / total
    merged_values = (sums_ref[:, LANES:] + jnp.dot(value_mix, arrived, preferred_element_type=F32)) / total
    merged_keys = merged_keys.astype(BF16)
    merged_values = merged_values.astype(BF16)
    merged_ref[0] = merged_keys
    merged_ref[1] = merged_values

    span = padded_ref.shape[0] // shards
    per_peer = span - 2
    scale = LANES ** (-0.5)
    bias = bias_ref[0:1, :]
    group = TILE * span
    peer, place = peer_place(rows_of((group, LANES)), span)
    lane = lanes_of((group, LANES))
    part = divided(lane, per_peer)
    diagonal = place == remainder(lane, per_peer)
    from_peer, from_place = peer_place(lanes_of((group, group)), span)
    to_peer, to_place = peer_place(rows_of((group, group)), span)
    gather = onehot((to_place == per_peer) & (from_peer == to_peer) & (from_place < per_peer))
    for at in range(0, padded_ref.shape[0], group):
        scores = lax.dot_general(
            padded_ref[at : at + group, :], merged_keys, (((1,), (1,)), ((), ())), preferred_element_type=F32
        )
        scores = scores * scale + bias
        peak = jnp.max(scores, axis=1, keepdims=True)
        prob = jnp.exp(scores - peak)
        size = jnp.sum(prob, axis=1, keepdims=True)
        sums = jnp.dot(prob.astype(BF16), merged_values, preferred_element_type=F32)
        stats = jnp.zeros((group, LANES), F32)
        for which, member in enumerate(split_parts(peak, PEAK_PARTS) + split_parts(size, SIZE_PARTS)):
            stats = jnp.where(part == which, member, stats)
        stats = jnp.where(diagonal, stats, 0.0).astype(BF16)
        stats = jnp.dot(gather, stats, preferred_element_type=F32)
        partial_ref[at : at + group, :] = jnp.where(place < per_peer, sums, stats).astype(BF16)


def combine_kernel(shards, partial_ref, finished_ref):
    count = partial_ref.shape[0]
    span = count // shards
    per_peer = span - 2
    partial = partial_ref[...]
    wide = (shards, count)
    picked = onehot(lanes_of(wide) == rows_of(wide) * span + per_peer)
    stats = jnp.dot(picked, partial, preferred_element_type=F32)

    def part(which):
        return pltpu.roll(stats, LANES - which * per_peer, 1) if which else stats

    valid = lanes_of((shards, LANES)) < per_peer
    peak = jnp.where(valid, (part(0) + part(1)) + part(2), 0.0)
    size = jnp.where(valid, part(3) + part(4), 1.0)
    rescale = jnp.exp(peak - jnp.max(peak, axis=0, keepdims=True))
    factor = rescale / jnp.sum(rescale * size, axis=0, keepdims=True)
    factor = jnp.concatenate([factor, jnp.zeros((LANES - shards, LANES), F32)], axis=0).T[:per_peer, :shards]
    factor = jnp.concatenate(split_parts(factor, 2), axis=0).astype(BF16)
    start = rows_of(wide) * span
    spread = onehot((lanes_of(wide) >= start) & (lanes_of(wide) < start + span))
    factor = jnp.dot(factor, spread, preferred_element_type=F32)
    unused, place = peer_place(lanes_of(factor.shape), span)
    factor = jnp.where(place == remainder(rows_of(factor.shape), per_peer), factor, 0.0).astype(BF16)
    total = jnp.dot(factor, partial, preferred_element_type=F32)
    finished = (total[:per_peer] + total[per_peer:]).astype(BF16)
    for peer in range(shards):
        finished_ref[peer] = finished


SMEM = pl.BlockSpec(memory_space=pltpu.SMEM)
VMEM = pl.BlockSpec(memory_space=pltpu.VMEM)
ANY = pl.BlockSpec(memory_space=pl.ANY)


def run_kernel(body, shards, shapes, specs, operands, pulled=()):
    scratch = [pltpu.VMEM(member.shape, member.dtype) for member in pulled]
    if pulled:
        scratch.append(pltpu.SemaphoreType.DMA((len(pulled),)))
    return pl.pallas_call(
        functools.partial(body, shards),
        out_shape=[jax.ShapeDtypeStruct(shape, dtype) for shape, dtype in shapes],
        in_specs=specs,
        out_specs=[VMEM] * len(shapes),
        scratch_shapes=scratch,
        compiler_params=pltpu.CompilerParams(vmem_limit_bytes=24 * 1024 * 1024),
    )(*operands)


def per_device(cache_keys, cache_values, importance, assignment, queries):
    row_count, head_dim = cache_keys.shape
    query_rows = queries.shape[0]
    heads = queries.shape[1] // head_dim
    shards = lax.axis_size("ctx")
    groups = lax.axis_size("kv")
    per_peer = query_rows * heads // shards
    span = per_peer + 2
    shard = lax.axis_index("ctx").astype(jnp.int32).reshape(1)
    assignment = assignment.reshape(1, row_count)

    slices = row_count // LANES
    (copies,) = run_kernel(copy_kernel, shards, [((groups * slices, LANES), BF16)], [VMEM], (importance,))
    importance = lax.all_to_all(copies.reshape(groups, slices, LANES), "kv", 0, 0, tiled=True)
    pulled = (assignment, cache_keys, cache_values)
    far, ahead, back, peer = run_kernel(
        rows_kernel,
        shards,
        [
            ((PIECES * shards, LANES), BF16),
            ((2 * NEAR, LANES), BF16),
            ((2 * NEAR, LANES), BF16),
            ((TILE, row_count), jnp.int32),
        ],
        [SMEM, ANY, ANY, ANY],
        (shard,) + pulled,
        pulled,
    )
    from_back = lax.ppermute(ahead, "ctx", [(i, (i + 1) % shards) for i in range(shards)])
    from_ahead = lax.ppermute(back, "ctx", [(i, (i - 1) % shards) for i in range(shards)])
    (far,) = run_kernel(
        weigh_kernel, shards, [((PIECES * shards, LANES), BF16)], [VMEM, VMEM, VMEM], (importance, peer, far)
    )
    far, importance = lax.optimization_barrier((far, importance))
    far = lax.all_to_all(far.reshape(shards, PIECES, LANES), "ctx", 0, 0, tiled=True)
    pulled = (assignment, cache_keys, cache_values, queries)
    sums, total, bias, padded = run_kernel(
        home_kernel,
        shards,
        [
            ((row_count, 2 * head_dim), F32),
            ((row_count, LANES), F32),
            ((TILE, row_count), F32),
            ((shards * span, head_dim), BF16),
        ],
        [SMEM, VMEM, ANY, ANY, ANY, ANY],
        (shard, importance) + pulled,
        pulled,
    )
    merged, partial = run_kernel(
        attend_kernel,
        shards,
        [((2, row_count, head_dim), BF16), ((shards * span, LANES), BF16)],
        [SMEM] + [VMEM] * 7,
        (shard, sums, total, bias, padded, far.reshape(shards * PIECES, LANES), from_back, from_ahead),
    )
    partial = lax.all_to_all(partial.reshape(shards, span // 2, 2, LANES), "ctx", 0, 0, tiled=True)
    merged_keys = merged[0]
    (finished,) = run_kernel(
        combine_kernel, shards, [((shards, per_peer, LANES), BF16)], [VMEM], (partial.reshape(shards * span, LANES),)
    )
    finished, merged, merged_keys = lax.optimization_barrier((finished, merged, merged_keys))
    finished = lax.all_to_all(finished, "ctx", 0, 0, tiled=True)
    merged_values = merged[1]
    tiles = query_rows // TILE
    attended = finished.reshape(tiles, heads, TILE, head_dim).transpose(0, 2, 1, 3)
    return (merged_keys, merged_values, attended.reshape(query_rows, heads * head_dim))


def solution(mesh):
    placed = (P("ctx", "kv"), P("ctx", "kv"), P("kv", "ctx"), P("ctx"), P(None, "kv"))
    return jax.shard_map(
        per_device,
        mesh=mesh,
        in_specs=placed,
        out_specs=(P("ctx", "kv"), P("ctx", "kv"), P(None, "kv")),
        check_vma=False,
    )
```

```python
import functools
import math

import jax
import jax.numpy as jnp
from jax import lax
from jax.experimental import pallas as pl
from jax.experimental.pallas import tpu as pltpu
from jax.sharding import PartitionSpec as P

NEAR = 16
LANES = 128
TILE = 8
PIECES = 4
NOTES = 2
FIRST_NUMBER = 32
PEAK_PARTS = 3
SIZE_PARTS = 2
SCORE_SCALE = LANES ** (-0.5) * math.log2(math.e)
F32 = jnp.float32
BF16 = jnp.bfloat16


def first_member(shards):
    return shards * FIRST_NUMBER // 64


def exchange(array, shards):
    first = first_member(shards)
    members = [(first + at) % shards for at in range(shards)]
    return lax.all_to_all(array, "ctx", 0, 0, tiled=True, axis_index_groups=[members])


def rows_of(shape):
    return lax.broadcasted_iota(jnp.int32, shape, 0)


def lanes_of(shape):
    return lax.broadcasted_iota(jnp.int32, shape, 1)


def onehot(flags):
    return flags.astype(F32).astype(BF16)


def row_weight(importance):
    summed = jnp.sum(importance.astype(F32), axis=0).astype(BF16).astype(F32)
    return jnp.concatenate([summed[at : at + 1, :] for at in range(summed.shape[0])], axis=1)


def split_parts(value, count):
    parts = []
    for _ in range(count):
        rounded = value.astype(BF16).astype(F32)
        parts.append(rounded)
        value = value - rounded
    return parts


def divided(index, size):
    if size & (size - 1):
        return (index * (-(-(1 << 16) // size))) >> 16
    return index >> (size.bit_length() - 1)


def remainder(index, size):
    if size & (size - 1):
        return index - divided(index, size) * size
    return index & (size - 1)


def peer_place(index, span):
    return divided(index, span), remainder(index, span)


def pull(sources, targets, semaphore):
    copies = [
        pltpu.make_async_copy(source, target, semaphore.at[at])
        for at, (source, target) in enumerate(zip(sources, targets))
    ]
    for copy in copies:
        copy.start()
    for copy in copies:
        copy.wait()


def position(shard, shards):
    moved = shard - first_member(shards)
    return jnp.where(moved < 0, moved + shards, moved)


def destination(shards, shard, assignment, row_count):
    owner = divided(assignment, row_count)
    distance = owner - shard
    distance = jnp.where(distance < 0, distance + shards, distance)
    ahead = distance == 1
    back = distance == shards - 1
    side = rows_of((TILE, row_count))
    flags = jnp.where(side == 0, ahead.astype(F32), jnp.where(side == 1, back.astype(F32), 0.0)).astype(BF16)
    earlier = onehot(rows_of((row_count, row_count)) < lanes_of((row_count, row_count)))
    ranks = jnp.dot(flags, earlier, preferred_element_type=F32).astype(jnp.int32)
    rank = jnp.where(ahead, ranks[0:1, :], jnp.where(back, ranks[1:2, :], 0))
    peer = jnp.where(distance == 0, -1, position(owner, shards))
    far_peer = jnp.where(ahead | back, -1, peer)
    return peer, far_peer, ahead, back, rank


def chosen_rows(shards, peer, far_peer, row_count):
    line = rows_of((PIECES * shards, row_count))
    return onehot(divided(line, PIECES) == jnp.where(remainder(line, PIECES) == NOTES, peer, far_peer))


def copy_kernel(shards, importance_ref, copies_ref):
    importance = importance_ref[...].astype(F32)
    slices = importance.shape[1] // LANES
    place = remainder(rows_of(copies_ref.shape), slices)
    copies = jnp.zeros(copies_ref.shape, F32)
    for at in range(slices):
        copies = jnp.where(place == at, importance[:, at * LANES : (at + 1) * LANES], copies)
    copies_ref[...] = copies.astype(BF16)


def rows_kernel(
    shards, shard_ref, assignment_hbm, keys_hbm, values_hbm, far_ref, first_ref, second_ref, peer_ref,
    assignment_ref, keys_ref, values_ref, semaphore,
):
    pull((assignment_hbm, keys_hbm, values_hbm), (assignment_ref, keys_ref, values_ref), semaphore)
    row_count = keys_ref.shape[0]
    assignment = assignment_ref[...]
    peer, far_peer, ahead, back, rank = destination(shards, shard_ref[0], assignment, row_count)
    rows = jnp.concatenate([keys_ref[...], values_ref[...]], axis=1)
    is_odd = remainder(shard_ref[0], 2)
    slot = jnp.where(ahead, is_odd * NEAR + rank, jnp.where(back, (1 - is_odd) * NEAR + rank, -1))
    near = jnp.dot(onehot(rows_of((2 * NEAR, row_count)) == slot), rows, preferred_element_type=F32).astype(BF16)
    first_ref[...] = jnp.concatenate([near[:NEAR, :LANES], near[:NEAR, LANES:]], axis=0)
    second_ref[...] = jnp.concatenate([near[NEAR:, :LANES], near[NEAR:, LANES:]], axis=0)
    chosen = chosen_rows(shards, peer, far_peer, row_count)
    picked = jnp.dot(chosen, rows, preferred_element_type=F32)
    target = remainder(assignment, row_count)
    part = rows_of((LANES, row_count))
    place = jnp.where(
        divided(part, NEAR) == 1,
        divided(target, LANES).astype(F32),
        jnp.where(divided(part, NEAR) == 2, remainder(target, LANES).astype(F32), 0.0),
    )
    notes = jnp.where(remainder(part, NEAR) == rank, place, 0.0).astype(BF16)
    noted = lax.dot_general(chosen, notes, (((1,), (1,)), ((), ())), preferred_element_type=F32)
    piece = remainder(rows_of((PIECES * shards, LANES)), PIECES)
    far_ref[...] = jnp.where(
        piece == 0, picked[:, :LANES], jnp.where(piece == 1, picked[:, LANES:], jnp.where(piece == NOTES, noted, 0.0))
    ).astype(BF16)
    at = rows_of((TILE, row_count))
    peer_ref[...] = jnp.where(at == 0, peer, jnp.where(at == 1, far_peer, rank))


def weigh_kernel(shards, importance_ref, peer_ref, far_ref, out_ref):
    row_count = peer_ref.shape[1]
    weight = row_weight(importance_ref[...])
    peer, far_peer, rank = peer_ref[0:1, :], peer_ref[1:2, :], peer_ref[2:3, :]
    chosen = chosen_rows(shards, peer, far_peer, row_count)
    notes = jnp.where(rows_of((LANES, row_count)) == rank, weight, 0.0).astype(BF16)
    noted = lax.dot_general(chosen, notes, (((1,), (1,)), ((), ())), preferred_element_type=F32)
    piece = remainder(rows_of((PIECES * shards, LANES)), PIECES)
    out_ref[...] = (far_ref[...].astype(F32) + jnp.where(piece == NOTES, noted, 0.0)).astype(BF16)


def home_kernel(
    shards, shard_ref, importance_ref, assignment_hbm, keys_hbm, values_hbm, queries_hbm,
    sums_ref, total_ref, bias_ref, padded_ref, assignment_ref, keys_ref, values_ref, queries_ref, semaphore,
):
    pull(
        (assignment_hbm, keys_hbm, values_hbm, queries_hbm),
        (assignment_ref, keys_ref, values_ref, queries_ref),
        semaphore,
    )
    row_count, head_dim = keys_ref.shape
    shard = shard_ref[0]
    assignment = assignment_ref[...]
    weight = row_weight(importance_ref[...])
    target = jnp.where(divided(assignment, row_count) == shard, remainder(assignment, row_count), -1)
    index = lanes_of((1, row_count))
    kept = target == index
    line = rows_of((row_count, row_count))
    mix = jnp.where(target == line, weight, jnp.where((index == line) & jnp.logical_not(kept), 1.0, 0.0)).astype(BF16)
    rows = jnp.concatenate([keys_ref[...], values_ref[...]], axis=1)
    sums_ref[...] = jnp.dot(mix, rows, preferred_element_type=F32)
    total_ref[...] = jnp.dot(mix, jnp.ones((row_count, LANES), BF16), preferred_element_type=F32)
    bias_ref[...] = jnp.broadcast_to(jnp.where(kept, 0.0, -jnp.inf), bias_ref.shape)

    query_rows = queries_ref.shape[0]
    heads = queries_ref.shape[1] // head_dim
    per_peer = query_rows * heads // shards
    span = per_peer + 2
    group = per_peer * heads
    peers = group // per_peer
    peer, place = peer_place(rows_of((peers * span, group)), span)
    per_tile = heads * TILE // per_peer
    head = remainder(peer, per_tile) * (per_peer // TILE) + divided(place, TILE)
    source = head * per_peer + divided(peer, per_tile) * TILE + remainder(place, TILE)
    order = onehot((source == lanes_of((peers * span, group))) & (place < per_peer))
    for part in range(query_rows // per_peer):
        block = queries_ref[part * per_peer : (part + 1) * per_peer, :]
        block = jnp.concatenate([block[:, at * head_dim : (at + 1) * head_dim] for at in range(heads)], axis=0)
        moved = jnp.dot(order, block, preferred_element_type=F32).astype(BF16)
        padded_ref[part * peers * span : (part + 1) * peers * span, :] = moved


def attend_kernel(
    shards, shard_ref, sums_ref, total_ref, bias_ref, padded_ref, far_ref, first_ref, second_ref,
    merged_ref, partial_ref,
):
    row_count = sums_ref.shape[0]
    shard = shard_ref[0]
    back = jnp.where(shard == 0, shards - 1, shard - 1)
    ahead = jnp.where(shard == shards - 1, 0, shard + 1)
    is_odd = remainder(shard, 2) == 1
    shard = position(shard, shards)
    first_source = position(jnp.where(is_odd, back, ahead), shards)
    second_source = position(jnp.where(is_odd, ahead, back), shards)

    far = far_ref[...]
    lines = PIECES * shards
    line = rows_of((lines, lines))
    piece = divided(line, shards)
    wanted = remainder(line, shards) * PIECES + piece
    neighbour = jnp.where(line == 3 * shards, first_source, second_source) * PIECES + NOTES
    wanted = jnp.where(piece < 3, wanted, jnp.where(line < 3 * shards + 2, neighbour, -1))
    pieces = jnp.dot(onehot(lanes_of((lines, lines)) == wanted), far, preferred_element_type=F32)
    notes = pieces[2 * shards : 3 * shards]
    if shards < LANES:
        notes = jnp.concatenate([notes, jnp.zeros((LANES - shards, LANES), F32)], axis=0)
    notes = notes.T
    near_notes = pieces[3 * shards : 3 * shards + TILE]
    near_target = (
        pltpu.roll(near_notes, LANES - NEAR, 1) * LANES + pltpu.roll(near_notes, LANES - 2 * NEAR, 1)
    )
    far_target = notes[NEAR : NEAR + 1, :] * LANES + notes[2 * NEAR : 2 * NEAR + 1, :]
    lane = lanes_of((1, LANES))
    near_start = [shards, shards + NEAR]
    is_far = (lane < shards) & (lane != first_source) & (lane != second_source) & (lane != shard)
    target = jnp.where(is_far, far_target, -1.0)
    weight = notes[0:1, :]
    for at, start in enumerate(near_start):
        inside = (lane >= start) & (lane < start + NEAR)
        target = jnp.where(inside, pltpu.roll(near_target, start, 1)[at : at + 1, :], target)
        weight = jnp.where(inside, pltpu.roll(near_notes, start, 1)[at : at + 1, :], weight)
    target = target.astype(jnp.int32)
    mix = jnp.where(target == rows_of((row_count, LANES)), weight, 0.0).astype(BF16)
    unused = jnp.zeros((LANES - shards - 2 * NEAR, 2 * LANES), BF16)
    arrived = jnp.concatenate(
        [jnp.concatenate([pieces[:shards], pieces[shards : 2 * shards]], axis=1).astype(BF16)]
        + [jnp.concatenate([near[:NEAR], near[NEAR:]], axis=1) for near in (first_ref[...], second_ref[...])]
        + [unused],
        axis=0,
    )
    total = total_ref[...] + jnp.dot(mix, jnp.ones((LANES, LANES), BF16), preferred_element_type=F32)
    sums = sums_ref[...] + jnp.dot(mix, arrived, preferred_element_type=F32)
    share = 1.0 / total
    merged_keys = (sums[:, :LANES] * share).astype(BF16)
    merged_values = (sums[:, LANES:] * share).astype(BF16)
    merged_ref[0] = merged_keys
    merged_ref[1] = merged_values

    span = padded_ref.shape[0] // shards
    per_peer = span - 2
    bias = bias_ref[0:1, :]
    group = TILE * span
    peer, place = peer_place(rows_of((group, LANES)), span)
    lane = lanes_of((group, LANES))
    diagonal = (place < per_peer) & (lane == peer * per_peer + place)
    inside = place < per_peer
    row = rows_of((TILE, LANES))
    peaks = jnp.zeros((TILE, LANES), F32)
    sizes = jnp.zeros((TILE, LANES), F32)
    starts = range(0, padded_ref.shape[0], group)
    for which, at in enumerate(starts):
        scores = lax.dot_general(
            padded_ref[at : at + group, :], merged_keys, (((1,), (1,)), ((), ())), preferred_element_type=F32
        )
        scores = scores + bias
        peak = jnp.max(scores, axis=1, keepdims=True)
        prob = jnp.exp2((scores - peak) * SCORE_SCALE)
        size = jnp.sum(prob, axis=1, keepdims=True)
        sums = jnp.dot(prob.astype(BF16), merged_values, preferred_element_type=F32)
        peaks = jnp.where(row == which, jnp.sum(jnp.where(diagonal, peak, 0.0), axis=0, keepdims=True), peaks)
        sizes = jnp.where(row == which, jnp.sum(jnp.where(diagonal, size, 0.0), axis=0, keepdims=True), sizes)
        partial_ref[at : at + group, :] = jnp.where(inside, sums, 0.0).astype(BF16)
    part = divided(lanes_of((TILE, LANES)), per_peer)
    members = split_parts(peaks, PEAK_PARTS) + split_parts(sizes, SIZE_PARTS)
    stats = []
    for turn in range(TILE):
        mine = jnp.zeros((TILE, LANES), F32)
        for which, member in enumerate(members):
            shift = (which - turn) * per_peer % LANES
            mine = jnp.where(part == which, pltpu.roll(member, shift, 1) if shift else member, mine)
        stats.append(mine)
    stats = jnp.concatenate(stats, axis=0).astype(BF16)
    peer, place = peer_place(rows_of((group, TILE * TILE)), span)
    source = lanes_of((group, TILE * TILE)) - jnp.where(place == per_peer, peer * TILE, -LANES)
    for which, at in enumerate(starts):
        spread = jnp.dot(onehot(source == which), stats, preferred_element_type=F32)
        partial_ref[at : at + group, :] = (partial_ref[at : at + group, :].astype(F32) + spread).astype(BF16)


def combine_kernel(shards, partial_ref, finished_ref):
    count = partial_ref.shape[0]
    span = count // shards
    per_peer = span - 2
    partial = partial_ref[...]
    wide = (shards, count)
    picked = onehot(lanes_of(wide) == rows_of(wide) * span + per_peer)
    stats = jnp.dot(picked, partial, preferred_element_type=F32)

    def part(which):
        return pltpu.roll(stats, LANES - which * per_peer, 1) if which else stats

    valid = lanes_of((shards, LANES)) < per_peer
    peak = jnp.where(valid, (part(0) + part(1)) + part(2), 0.0)
    size = jnp.where(valid, part(3) + part(4), 1.0)
    rescale = jnp.exp2((peak - jnp.max(peak, axis=0, keepdims=True)) * SCORE_SCALE)
    factor = rescale / jnp.sum(rescale * size, axis=0, keepdims=True)
    factor = jnp.concatenate([factor, jnp.zeros((LANES - shards, LANES), F32)], axis=0).T[:per_peer, :shards]
    factor = jnp.concatenate(split_parts(factor, 2), axis=0).astype(BF16)
    start = rows_of(wide) * span
    spread = onehot((lanes_of(wide) >= start) & (lanes_of(wide) < start + span))
    factor = jnp.dot(factor, spread, preferred_element_type=F32)
    unused, place = peer_place(lanes_of(factor.shape), span)
    factor = jnp.where(place == remainder(rows_of(factor.shape), per_peer), factor, 0.0).astype(BF16)
    total = jnp.dot(factor, partial, preferred_element_type=F32)
    finished = (total[:per_peer] + total[per_peer:]).astype(BF16)
    for peer in range(shards):
        finished_ref[peer] = finished


SMEM = pl.BlockSpec(memory_space=pltpu.SMEM)
VMEM = pl.BlockSpec(memory_space=pltpu.VMEM)
ANY = pl.BlockSpec(memory_space=pl.ANY)


def run_kernel(body, shards, shapes, specs, operands, pulled=()):
    scratch = [pltpu.VMEM(member.shape, member.dtype) for member in pulled]
    if pulled:
        scratch.append(pltpu.SemaphoreType.DMA((len(pulled),)))
    return pl.pallas_call(
        functools.partial(body, shards),
        out_shape=[jax.ShapeDtypeStruct(shape, dtype) for shape, dtype in shapes],
        in_specs=specs,
        out_specs=[VMEM] * len(shapes),
        scratch_shapes=scratch,
        compiler_params=pltpu.CompilerParams(vmem_limit_bytes=24 * 1024 * 1024),
    )(*operands)


def per_device(cache_keys, cache_values, importance, assignment, queries):
    row_count, head_dim = cache_keys.shape
    query_rows = queries.shape[0]
    heads = queries.shape[1] // head_dim
    shards = lax.axis_size("ctx")
    groups = lax.axis_size("kv")
    per_peer = query_rows * heads // shards
    span = per_peer + 2
    shard = lax.axis_index("ctx").astype(jnp.int32).reshape(1)
    assignment = assignment.reshape(1, row_count)

    slices = row_count // LANES
    (copies,) = run_kernel(copy_kernel, shards, [((groups * slices, LANES), BF16)], [VMEM], (importance,))
    importance = lax.all_to_all(copies.reshape(groups, slices, LANES), "kv", 0, 0, tiled=True)
    pulled = (assignment, cache_keys, cache_values)
    far, first, second, peer = run_kernel(
        rows_kernel,
        shards,
        [
            ((PIECES * shards, LANES), BF16),
            ((2 * NEAR, LANES), BF16),
            ((2 * NEAR, LANES), BF16),
            ((TILE, row_count), jnp.int32),
        ],
        [SMEM, ANY, ANY, ANY],
        (shard,) + pulled,
        pulled,
    )
    first = lax.ppermute(first, "ctx", [(i, (i + 1 - 2 * (i % 2)) % shards) for i in range(shards)])
    second = lax.ppermute(second, "ctx", [(i, (i - 1 + 2 * (i % 2)) % shards) for i in range(shards)])
    (far,) = run_kernel(
        weigh_kernel, shards, [((PIECES * shards, LANES), BF16)], [VMEM, VMEM, VMEM], (importance, peer, far)
    )
    far, importance = lax.optimization_barrier((far, importance))
    far = exchange(far.reshape(shards, PIECES, LANES), shards)
    pulled = (assignment, cache_keys, cache_values, queries)
    sums, total, bias, padded = run_kernel(
        home_kernel,
        shards,
        [
            ((row_count, 2 * head_dim), F32),
            ((row_count, LANES), F32),
            ((TILE, row_count), F32),
            ((shards * span, head_dim), BF16),
        ],
        [SMEM, VMEM, ANY, ANY, ANY, ANY],
        (shard, importance) + pulled,
        pulled,
    )
    merged, partial = run_kernel(
        attend_kernel,
        shards,
        [((2, row_count, head_dim), BF16), ((shards * span, LANES), BF16)],
        [SMEM] + [VMEM] * 7,
        (shard, sums, total, bias, padded, far.reshape(shards * PIECES, LANES), first, second),
    )
    partial = exchange(partial.reshape(shards, span // 2, 2, LANES), shards)
    merged_keys = merged[0]
    (finished,) = run_kernel(
        combine_kernel, shards, [((shards, per_peer, LANES), BF16)], [VMEM], (partial.reshape(shards * span, LANES),)
    )
    finished, merged, merged_keys = lax.optimization_barrier((finished, merged, merged_keys))
    finished = exchange(finished, shards)
    merged_values = merged[1]
    tiles = query_rows // TILE
    attended = finished.reshape(tiles, heads, TILE, head_dim).transpose(0, 2, 1, 3)
    return (merged_keys, merged_values, attended.reshape(query_rows, heads * head_dim))


def solution(mesh):
    placed = (P("ctx", "kv"), P("ctx", "kv"), P("kv", "ctx"), P("ctx"), P(None, "kv"))
    return jax.shard_map(
        per_device,
        mesh=mesh,
        in_specs=placed,
        out_specs=(P("ctx", "kv"), P("ctx", "kv"), P(None, "kv")),
        check_vma=False,
    )
```

```python
import functools
import math

import jax
import jax.numpy as jnp
from jax import lax
from jax.experimental import pallas as pl
from jax.experimental.pallas import tpu as pltpu
from jax.sharding import PartitionSpec as P

NEAR = 16
LANES = 128
TILE = 8
PIECES = 4
NOTES = 2
FIRST_NUMBER = 43
PEAK_PARTS = 3
SIZE_PARTS = 2
SCORE_SCALE = LANES ** (-0.5) * math.log2(math.e)
F32 = jnp.float32
BF16 = jnp.bfloat16


def first_member(shards):
    return shards * FIRST_NUMBER // 64


def exchange(array, shards):
    first = first_member(shards)
    members = [(first + at) % shards for at in range(shards)]
    return lax.all_to_all(array, "ctx", 0, 0, tiled=True, axis_index_groups=[members])


def rows_of(shape):
    return lax.broadcasted_iota(jnp.int32, shape, 0)


def lanes_of(shape):
    return lax.broadcasted_iota(jnp.int32, shape, 1)


def onehot(flags):
    return flags.astype(F32).astype(BF16)


def row_weight(importance):
    summed = jnp.sum(importance.astype(F32), axis=0).astype(BF16).astype(F32)
    return jnp.concatenate([summed[at : at + 1, :] for at in range(summed.shape[0])], axis=1)


def split_parts(value, count):
    parts = []
    for _ in range(count):
        rounded = value.astype(BF16).astype(F32)
        parts.append(rounded)
        value = value - rounded
    return parts


def divided(index, size):
    if size & (size - 1):
        return (index * (-(-(1 << 16) // size))) >> 16
    return index >> (size.bit_length() - 1)


def remainder(index, size):
    if size & (size - 1):
        return index - divided(index, size) * size
    return index & (size - 1)


def peer_place(index, span):
    return divided(index, span), remainder(index, span)


def pull(sources, targets, semaphore):
    copies = [
        pltpu.make_async_copy(source, target, semaphore.at[at])
        for at, (source, target) in enumerate(zip(sources, targets))
    ]
    for copy in copies:
        copy.start()
    for copy in copies:
        copy.wait()


def position(shard, shards):
    moved = shard - first_member(shards)
    return jnp.where(moved < 0, moved + shards, moved)


def destination(shards, shard, assignment, row_count):
    owner = divided(assignment, row_count)
    distance = owner - shard
    distance = jnp.where(distance < 0, distance + shards, distance)
    ahead = distance == 1
    back = distance == shards - 1
    side = rows_of((TILE, row_count))
    flags = jnp.where(side == 0, ahead.astype(F32), jnp.where(side == 1, back.astype(F32), 0.0)).astype(BF16)
    earlier = onehot(rows_of((row_count, row_count)) < lanes_of((row_count, row_count)))
    ranks = jnp.dot(flags, earlier, preferred_element_type=F32).astype(jnp.int32)
    rank = jnp.where(ahead, ranks[0:1, :], jnp.where(back, ranks[1:2, :], 0))
    peer = jnp.where(distance == 0, -1, position(owner, shards))
    far_peer = jnp.where(ahead | back, -1, peer)
    return peer, far_peer, ahead, back, rank


def chosen_rows(shards, peer, far_peer, row_count):
    line = rows_of((PIECES * shards, row_count))
    return onehot(divided(line, PIECES) == jnp.where(remainder(line, PIECES) == NOTES, peer, far_peer))


def copy_kernel(shards, importance_hbm, copies_ref, importance_ref, semaphore):
    pull((importance_hbm,), (importance_ref,), semaphore)
    importance = importance_ref[...].astype(F32)
    slices = importance.shape[1] // LANES
    place = remainder(rows_of(copies_ref.shape), slices)
    copies = jnp.zeros(copies_ref.shape, F32)
    for at in range(slices):
        copies = jnp.where(place == at, importance[:, at * LANES : (at + 1) * LANES], copies)
    copies_ref[...] = copies.astype(BF16)


def rows_kernel(
    shards, shard_ref, assignment_hbm, keys_hbm, values_hbm, far_ref, first_ref, second_ref, peer_ref,
    assignment_ref, keys_ref, values_ref, semaphore,
):
    pull((assignment_hbm, keys_hbm, values_hbm), (assignment_ref, keys_ref, values_ref), semaphore)
    row_count = keys_ref.shape[0]
    assignment = assignment_ref[...]
    peer, far_peer, ahead, back, rank = destination(shards, shard_ref[0], assignment, row_count)
    rows = jnp.concatenate([keys_ref[...], values_ref[...]], axis=1)
    is_even = 1 - remainder(shard_ref[0], 2)
    slot = jnp.where(ahead, is_even * NEAR + rank, jnp.where(back, (1 - is_even) * NEAR + rank, -1))
    near = jnp.dot(onehot(rows_of((2 * NEAR, row_count)) == slot), rows, preferred_element_type=F32).astype(BF16)
    first_ref[...] = jnp.concatenate([near[:NEAR, :LANES], near[:NEAR, LANES:]], axis=0)
    second_ref[...] = jnp.concatenate([near[NEAR:, :LANES], near[NEAR:, LANES:]], axis=0)
    chosen = chosen_rows(shards, peer, far_peer, row_count)
    picked = jnp.dot(chosen, rows, preferred_element_type=F32)
    target = remainder(assignment, row_count)
    part = rows_of((LANES, row_count))
    place = jnp.where(
        divided(part, NEAR) == 1,
        divided(target, LANES).astype(F32),
        jnp.where(divided(part, NEAR) == 2, remainder(target, LANES).astype(F32), 0.0),
    )
    notes = jnp.where(remainder(part, NEAR) == rank, place, 0.0).astype(BF16)
    noted = lax.dot_general(chosen, notes, (((1,), (1,)), ((), ())), preferred_element_type=F32)
    piece = remainder(rows_of((PIECES * shards, LANES)), PIECES)
    far_ref[...] = jnp.where(
        piece == 0, picked[:, :LANES], jnp.where(piece == 1, picked[:, LANES:], jnp.where(piece == NOTES, noted, 0.0))
    ).astype(BF16)
    at = rows_of((TILE, row_count))
    peer_ref[...] = jnp.where(at == 0, peer, jnp.where(at == 1, far_peer, rank))


def weigh_kernel(shards, importance_ref, peer_ref, far_ref, out_ref):
    row_count = peer_ref.shape[1]
    weight = row_weight(importance_ref[...])
    peer, far_peer, rank = peer_ref[0:1, :], peer_ref[1:2, :], peer_ref[2:3, :]
    chosen = chosen_rows(shards, peer, far_peer, row_count)
    notes = jnp.where(rows_of((LANES, row_count)) == rank, weight, 0.0).astype(BF16)
    noted = lax.dot_general(chosen, notes, (((1,), (1,)), ((), ())), preferred_element_type=F32)
    piece = remainder(rows_of((PIECES * shards, LANES)), PIECES)
    out_ref[...] = (far_ref[...].astype(F32) + jnp.where(piece == NOTES, noted, 0.0)).astype(BF16)


def home_kernel(
    shards, shard_ref, importance_ref, assignment_hbm, keys_hbm, values_hbm, queries_hbm,
    sums_ref, total_ref, bias_ref, padded_ref, assignment_ref, keys_ref, values_ref, queries_ref, semaphore,
):
    pull(
        (assignment_hbm, keys_hbm, values_hbm, queries_hbm),
        (assignment_ref, keys_ref, values_ref, queries_ref),
        semaphore,
    )
    row_count, head_dim = keys_ref.shape
    shard = shard_ref[0]
    assignment = assignment_ref[...]
    weight = row_weight(importance_ref[...])
    target = jnp.where(divided(assignment, row_count) == shard, remainder(assignment, row_count), -1)
    index = lanes_of((1, row_count))
    kept = target == index
    line = rows_of((row_count, row_count))
    mix = jnp.where(target == line, weight, jnp.where((index == line) & jnp.logical_not(kept), 1.0, 0.0)).astype(BF16)
    rows = jnp.concatenate([keys_ref[...], values_ref[...]], axis=1)
    sums_ref[...] = jnp.dot(mix, rows, preferred_element_type=F32)
    total_ref[...] = jnp.dot(mix, jnp.ones((row_count, LANES), BF16), preferred_element_type=F32)
    bias_ref[...] = jnp.broadcast_to(jnp.where(kept, 0.0, -jnp.inf), bias_ref.shape)

    query_rows = queries_ref.shape[0]
    heads = queries_ref.shape[1] // head_dim
    per_peer = query_rows * heads // shards
    span = per_peer + 2
    group = per_peer * heads
    peers = group // per_peer
    peer, place = peer_place(rows_of((peers * span, group)), span)
    per_tile = heads * TILE // per_peer
    head = remainder(peer, per_tile) * (per_peer // TILE) + divided(place, TILE)
    source = head * per_peer + divided(peer, per_tile) * TILE + remainder(place, TILE)
    order = onehot((source == lanes_of((peers * span, group))) & (place < per_peer))
    for part in range(query_rows // per_peer):
        block = queries_ref[part * per_peer : (part + 1) * per_peer, :]
        block = jnp.concatenate([block[:, at * head_dim : (at + 1) * head_dim] for at in range(heads)], axis=0)
        moved = jnp.dot(order, block, preferred_element_type=F32).astype(BF16)
        padded_ref[part * peers * span : (part + 1) * peers * span, :] = moved


def attend_kernel(
    shards, shard_ref, sums_ref, total_ref, bias_ref, padded_ref, far_ref, first_ref, second_ref,
    merged_keys_ref, merged_values_ref, partial_ref,
):
    row_count = sums_ref.shape[0]
    shard = shard_ref[0]
    back = jnp.where(shard == 0, shards - 1, shard - 1)
    ahead = jnp.where(shard == shards - 1, 0, shard + 1)
    is_odd = remainder(shard, 2) == 1
    shard = position(shard, shards)
    first_source = position(jnp.where(is_odd, ahead, back), shards)
    second_source = position(jnp.where(is_odd, back, ahead), shards)

    far = far_ref[...]
    lines = PIECES * shards
    line = rows_of((lines, lines))
    piece = divided(line, shards)
    wanted = remainder(line, shards) * PIECES + piece
    neighbour = jnp.where(line == 3 * shards, first_source, second_source) * PIECES + NOTES
    wanted = jnp.where(piece < 3, wanted, jnp.where(line < 3 * shards + 2, neighbour, -1))
    pieces = jnp.dot(onehot(lanes_of((lines, lines)) == wanted), far, preferred_element_type=F32)
    notes = pieces[2 * shards : 3 * shards]
    if shards < LANES:
        notes = jnp.concatenate([notes, jnp.zeros((LANES - shards, LANES), F32)], axis=0)
    notes = notes.T
    near_notes = pieces[3 * shards : 3 * shards + TILE]
    near_target = (
        pltpu.roll(near_notes, LANES - NEAR, 1) * LANES + pltpu.roll(near_notes, LANES - 2 * NEAR, 1)
    )
    far_target = notes[NEAR : NEAR + 1, :] * LANES + notes[2 * NEAR : 2 * NEAR + 1, :]
    lane = lanes_of((1, LANES))
    near_start = [shards, shards + NEAR]
    is_far = (lane < shards) & (lane != first_source) & (lane != second_source) & (lane != shard)
    target = jnp.where(is_far, far_target, -1.0)
    weight = notes[0:1, :]
    for at, start in enumerate(near_start):
        inside = (lane >= start) & (lane < start + NEAR)
        target = jnp.where(inside, pltpu.roll(near_target, start, 1)[at : at + 1, :], target)
        weight = jnp.where(inside, pltpu.roll(near_notes, start, 1)[at : at + 1, :], weight)
    target = target.astype(jnp.int32)
    mix = jnp.where(target == rows_of((row_count, LANES)), weight, 0.0).astype(BF16)
    unused = jnp.zeros((LANES - shards - 2 * NEAR, 2 * LANES), BF16)
    arrived = jnp.concatenate(
        [jnp.concatenate([pieces[:shards], pieces[shards : 2 * shards]], axis=1).astype(BF16)]
        + [jnp.concatenate([near[:NEAR], near[NEAR:]], axis=1) for near in (first_ref[...], second_ref[...])]
        + [unused],
        axis=0,
    )
    total = total_ref[...] + jnp.dot(mix, jnp.ones((LANES, LANES), BF16), preferred_element_type=F32)
    sums = sums_ref[...] + jnp.dot(mix, arrived, preferred_element_type=F32)
    share = 1.0 / total
    merged_keys = (sums[:, :LANES] * share).astype(BF16)
    merged_values = (sums[:, LANES:] * share).astype(BF16)
    merged_keys_ref[...] = merged_keys
    merged_values_ref[...] = merged_values

    span = padded_ref.shape[0] // shards
    per_peer = span - 2
    bias = bias_ref[0:1, :]
    group = TILE * span
    peer, place = peer_place(rows_of((group, LANES)), span)
    lane = lanes_of((group, LANES))
    diagonal = (place < per_peer) & (lane == peer * per_peer + place)
    inside = place < per_peer
    row = rows_of((TILE, LANES))
    peaks = jnp.zeros((TILE, LANES), F32)
    sizes = jnp.zeros((TILE, LANES), F32)
    starts = range(0, padded_ref.shape[0], group)
    for which, at in enumerate(starts):
        scores = lax.dot_general(
            padded_ref[at : at + group, :], merged_keys, (((1,), (1,)), ((), ())), preferred_element_type=F32
        )
        scores = scores + bias
        peak = jnp.max(scores, axis=1, keepdims=True)
        prob = jnp.exp2((scores - peak) * SCORE_SCALE)
        size = jnp.sum(prob, axis=1, keepdims=True)
        sums = jnp.dot(prob.astype(BF16), merged_values, preferred_element_type=F32)
        peaks = jnp.where(row == which, jnp.sum(jnp.where(diagonal, peak, 0.0), axis=0, keepdims=True), peaks)
        sizes = jnp.where(row == which, jnp.sum(jnp.where(diagonal, size, 0.0), axis=0, keepdims=True), sizes)
        partial_ref[at : at + group, :] = jnp.where(inside, sums, 0.0).astype(BF16)
    part = divided(lanes_of((TILE, LANES)), per_peer)
    members = split_parts(peaks, PEAK_PARTS) + split_parts(sizes, SIZE_PARTS)
    stats = []
    for turn in range(TILE):
        mine = jnp.zeros((TILE, LANES), F32)
        for which, member in enumerate(members):
            shift = (which - turn) * per_peer % LANES
            mine = jnp.where(part == which, pltpu.roll(member, shift, 1) if shift else member, mine)
        stats.append(mine)
    stats = jnp.concatenate(stats, axis=0).astype(BF16)
    peer, place = peer_place(rows_of((group, TILE * TILE)), span)
    source = lanes_of((group, TILE * TILE)) - jnp.where(place == per_peer, peer * TILE, -LANES)
    for which, at in enumerate(starts):
        spread = jnp.dot(onehot(source == which), stats, preferred_element_type=F32)
        partial_ref[at : at + group, :] = (partial_ref[at : at + group, :].astype(F32) + spread).astype(BF16)


def combine_kernel(shards, partial_ref, finished_ref):
    count = partial_ref.shape[0]
    span = count // shards
    per_peer = span - 2
    partial = partial_ref[...]
    wide = (shards, count)
    picked = onehot(lanes_of(wide) == rows_of(wide) * span + per_peer)
    stats = jnp.dot(picked, partial, preferred_element_type=F32)

    def part(which):
        return pltpu.roll(stats, LANES - which * per_peer, 1) if which else stats

    valid = lanes_of((shards, LANES)) < per_peer
    peak = jnp.where(valid, (part(0) + part(1)) + part(2), 0.0)
    size = jnp.where(valid, part(3) + part(4), 1.0)
    rescale = jnp.exp2((peak - jnp.max(peak, axis=0, keepdims=True)) * SCORE_SCALE)
    factor = rescale / jnp.sum(rescale * size, axis=0, keepdims=True)
    factor = jnp.concatenate([factor, jnp.zeros((LANES - shards, LANES), F32)], axis=0).T[:per_peer, :shards]
    factor = jnp.concatenate(split_parts(factor, 2), axis=0).astype(BF16)
    start = rows_of(wide) * span
    spread = onehot((lanes_of(wide) >= start) & (lanes_of(wide) < start + span))
    factor = jnp.dot(factor, spread, preferred_element_type=F32)
    unused, place = peer_place(lanes_of(factor.shape), span)
    factor = jnp.where(place == remainder(rows_of(factor.shape), per_peer), factor, 0.0).astype(BF16)
    total = jnp.dot(factor, partial, preferred_element_type=F32)
    finished = (total[:per_peer] + total[per_peer:]).astype(BF16)
    for peer in range(shards):
        finished_ref[peer] = finished


SMEM = pl.BlockSpec(memory_space=pltpu.SMEM)
VMEM = pl.BlockSpec(memory_space=pltpu.VMEM)
HBM = pl.BlockSpec(memory_space=pltpu.HBM)


def run_kernel(body, shards, shapes, specs, operands, pulled=()):
    scratch = [pltpu.VMEM(member.shape, member.dtype) for member in pulled]
    if pulled:
        scratch.append(pltpu.SemaphoreType.DMA((len(pulled),)))
    return pl.pallas_call(
        functools.partial(body, shards),
        out_shape=[jax.ShapeDtypeStruct(shape, dtype) for shape, dtype in shapes],
        in_specs=specs,
        out_specs=[VMEM] * len(shapes),
        scratch_shapes=scratch,
        compiler_params=pltpu.CompilerParams(vmem_limit_bytes=24 * 1024 * 1024),
    )(*operands)


def per_device(cache_keys, cache_values, importance, assignment, queries):
    row_count, head_dim = cache_keys.shape
    query_rows = queries.shape[0]
    heads = queries.shape[1] // head_dim
    shards = lax.axis_size("ctx")
    groups = lax.axis_size("kv")
    per_peer = query_rows * heads // shards
    span = per_peer + 2
    shard = lax.axis_index("ctx").astype(jnp.int32).reshape(1)
    assignment = assignment.reshape(1, row_count)

    slices = row_count // LANES
    pulled = (importance,)
    (copies,) = run_kernel(copy_kernel, shards, [((groups * slices, LANES), BF16)], [HBM], pulled, pulled)
    importance = lax.all_to_all(copies.reshape(groups, slices, LANES), "kv", 0, 0, tiled=True)
    pulled = (assignment, cache_keys, cache_values)
    far, first, second, peer = run_kernel(
        rows_kernel,
        shards,
        [
            ((PIECES * shards, LANES), BF16),
            ((2 * NEAR, LANES), BF16),
            ((2 * NEAR, LANES), BF16),
            ((TILE, row_count), jnp.int32),
        ],
        [SMEM, HBM, HBM, HBM],
        (shard,) + pulled,
        pulled,
    )
    first = lax.ppermute(first, "ctx", [(i, (i - 1 + 2 * (i % 2)) % shards) for i in range(shards)])
    second = lax.ppermute(second, "ctx", [(i, (i + 1 - 2 * (i % 2)) % shards) for i in range(shards)])
    (far,) = run_kernel(
        weigh_kernel, shards, [((PIECES * shards, LANES), BF16)], [VMEM, VMEM, VMEM], (importance, peer, far)
    )
    far, importance = lax.optimization_barrier((far, importance))
    far = exchange(far.reshape(shards, PIECES, LANES), shards)
    pulled = (assignment, cache_keys, cache_values, queries)
    sums, total, bias, padded = run_kernel(
        home_kernel,
        shards,
        [
            ((row_count, 2 * head_dim), F32),
            ((row_count, LANES), F32),
            ((TILE, row_count), F32),
            ((shards * span, head_dim), BF16),
        ],
        [SMEM, VMEM, HBM, HBM, HBM, HBM],
        (shard, importance) + pulled,
        pulled,
    )
    merged_keys, merged_values, partial = run_kernel(
        attend_kernel,
        shards,
        [(cache_keys.shape, BF16), (cache_keys.shape, BF16), ((shards * span, LANES), BF16)],
        [SMEM] + [VMEM] * 7,
        (shard, sums, total, bias, padded, far.reshape(shards * PIECES, LANES), first, second),
    )
    partial = exchange(partial.reshape(shards, span // 2, 2, LANES), shards)
    (finished,) = run_kernel(
        combine_kernel, shards, [((shards, per_peer, LANES), BF16)], [VMEM], (partial.reshape(shards * span, LANES),)
    )
    finished = exchange(finished, shards)
    tiles = query_rows // TILE
    attended = finished.reshape(tiles, heads, TILE, head_dim).transpose(0, 2, 1, 3)
    return (merged_keys, merged_values, attended.reshape(query_rows, heads * head_dim))


def solution(mesh):
    placed = (P("ctx", "kv"), P("ctx", "kv"), P("kv", "ctx"), P("ctx"), P(None, "kv"))
    return jax.shard_map(
        per_device,
        mesh=mesh,
        in_specs=placed,
        out_specs=(P("ctx", "kv"), P("ctx", "kv"), P(None, "kv")),
        check_vma=False,
    )
```

```python
import functools
import math

import jax
import jax.numpy as jnp
from jax import lax
from jax.experimental import pallas as pl
from jax.experimental.pallas import tpu as pltpu
from jax.sharding import PartitionSpec as P

NEAR = 16
LANES = 128
TILE = 8
PIECES = 4
NOTES = 2
ROWS_FIRST = (11, 43)
SUMS_FIRST = (43, 43)
PEAK_PARTS = 3
SIZE_PARTS = 2
SCORE_SCALE = LANES ** (-0.5) * math.log2(math.e)
F32 = jnp.float32
BF16 = jnp.bfloat16


def exchange(array, shards, groups, firsts):
    members = []
    for group in range(groups):
        first = shards * firsts[group % 2] // 64
        members.append([(first + at) % shards * groups + group for at in range(shards)])
    return lax.all_to_all(array, ("ctx", "kv"), 0, 0, tiled=True, axis_index_groups=members)


def rows_of(shape):
    return lax.broadcasted_iota(jnp.int32, shape, 0)


def lanes_of(shape):
    return lax.broadcasted_iota(jnp.int32, shape, 1)


def onehot(flags):
    return flags.astype(F32).astype(BF16)


def row_weight(importance):
    summed = jnp.sum(importance.astype(F32), axis=0).astype(BF16).astype(F32)
    return jnp.concatenate([summed[at : at + 1, :] for at in range(summed.shape[0])], axis=1)


def split_parts(value, count):
    parts = []
    for _ in range(count):
        rounded = value.astype(BF16).astype(F32)
        parts.append(rounded)
        value = value - rounded
    return parts


def divided(index, size):
    if size & (size - 1):
        return (index * (-(-(1 << 16) // size))) >> 16
    return index >> (size.bit_length() - 1)


def remainder(index, size):
    if size & (size - 1):
        return index - divided(index, size) * size
    return index & (size - 1)


def peer_place(index, span):
    return divided(index, span), remainder(index, span)


def pull(sources, targets, semaphore):
    copies = [
        pltpu.make_async_copy(source, target, semaphore.at[at])
        for at, (source, target) in enumerate(zip(sources, targets))
    ]
    for copy in copies:
        copy.start()
    for copy in copies:
        copy.wait()


def position(shard, first, shards):
    moved = shard - first
    return jnp.where(moved < 0, moved + shards, moved)


def destination(shards, shard, first, assignment, row_count):
    owner = divided(assignment, row_count)
    distance = owner - shard
    distance = jnp.where(distance < 0, distance + shards, distance)
    ahead = distance == 1
    back = distance == shards - 1
    side = rows_of((TILE, row_count))
    flags = jnp.where(side == 0, ahead.astype(F32), jnp.where(side == 1, back.astype(F32), 0.0)).astype(BF16)
    earlier = onehot(rows_of((row_count, row_count)) < lanes_of((row_count, row_count)))
    ranks = jnp.dot(flags, earlier, preferred_element_type=F32).astype(jnp.int32)
    rank = jnp.where(ahead, ranks[0:1, :], jnp.where(back, ranks[1:2, :], 0))
    peer = jnp.where(distance == 0, -1, position(owner, first, shards))
    far_peer = jnp.where(ahead | back, -1, peer)
    return peer, far_peer, ahead, back, rank


def chosen_rows(shards, peer, far_peer, row_count):
    line = rows_of((PIECES * shards, row_count))
    return onehot(divided(line, PIECES) == jnp.where(remainder(line, PIECES) == NOTES, peer, far_peer))


def copy_kernel(shards, importance_hbm, copies_ref, importance_ref, semaphore):
    pull((importance_hbm,), (importance_ref,), semaphore)
    importance = importance_ref[...].astype(F32)
    slices = importance.shape[1] // LANES
    place = remainder(rows_of(copies_ref.shape), slices)
    copies = jnp.zeros(copies_ref.shape, F32)
    for at in range(slices):
        copies = jnp.where(place == at, importance[:, at * LANES : (at + 1) * LANES], copies)
    copies_ref[...] = copies.astype(BF16)


def rows_kernel(
    shards, shard_ref, begin_ref, assignment_hbm, keys_hbm, values_hbm, far_ref, first_ref, second_ref, peer_ref,
    assignment_ref, keys_ref, values_ref, semaphore,
):
    pull((assignment_hbm, keys_hbm, values_hbm), (assignment_ref, keys_ref, values_ref), semaphore)
    row_count = keys_ref.shape[0]
    assignment = assignment_ref[...]
    peer, far_peer, ahead, back, rank = destination(shards, shard_ref[0], begin_ref[0], assignment, row_count)
    rows = jnp.concatenate([keys_ref[...], values_ref[...]], axis=1)
    is_even = 1 - remainder(shard_ref[0], 2)
    slot = jnp.where(ahead, is_even * NEAR + rank, jnp.where(back, (1 - is_even) * NEAR + rank, -1))
    near = jnp.dot(onehot(rows_of((2 * NEAR, row_count)) == slot), rows, preferred_element_type=F32).astype(BF16)
    first_ref[...] = jnp.concatenate([near[:NEAR, :LANES], near[:NEAR, LANES:]], axis=0)
    second_ref[...] = jnp.concatenate([near[NEAR:, :LANES], near[NEAR:, LANES:]], axis=0)
    chosen = chosen_rows(shards, peer, far_peer, row_count)
    picked = jnp.dot(chosen, rows, preferred_element_type=F32)
    target = remainder(assignment, row_count)
    part = rows_of((LANES, row_count))
    place = jnp.where(
        divided(part, NEAR) == 1,
        divided(target, LANES).astype(F32),
        jnp.where(divided(part, NEAR) == 2, remainder(target, LANES).astype(F32), 0.0),
    )
    notes = jnp.where(remainder(part, NEAR) == rank, place, 0.0).astype(BF16)
    noted = lax.dot_general(chosen, notes, (((1,), (1,)), ((), ())), preferred_element_type=F32)
    piece = remainder(rows_of((PIECES * shards, LANES)), PIECES)
    far_ref[...] = jnp.where(
        piece == 0, picked[:, :LANES], jnp.where(piece == 1, picked[:, LANES:], jnp.where(piece == NOTES, noted, 0.0))
    ).astype(BF16)
    at = rows_of((TILE, row_count))
    peer_ref[...] = jnp.where(at == 0, peer, jnp.where(at == 1, far_peer, rank))


def weigh_kernel(shards, importance_ref, peer_ref, far_ref, out_ref):
    row_count = peer_ref.shape[1]
    weight = row_weight(importance_ref[...])
    peer, far_peer, rank = peer_ref[0:1, :], peer_ref[1:2, :], peer_ref[2:3, :]
    chosen = chosen_rows(shards, peer, far_peer, row_count)
    notes = jnp.where(rows_of((LANES, row_count)) == rank, weight, 0.0).astype(BF16)
    noted = lax.dot_general(chosen, notes, (((1,), (1,)), ((), ())), preferred_element_type=F32)
    piece = remainder(rows_of((PIECES * shards, LANES)), PIECES)
    out_ref[...] = (far_ref[...].astype(F32) + jnp.where(piece == NOTES, noted, 0.0)).astype(BF16)


def home_kernel(
    shards, shard_ref, importance_ref, assignment_hbm, keys_hbm, values_hbm, queries_hbm,
    sums_ref, total_ref, bias_ref, padded_ref, assignment_ref, keys_ref, values_ref, queries_ref, semaphore,
):
    pull(
        (assignment_hbm, keys_hbm, values_hbm, queries_hbm),
        (assignment_ref, keys_ref, values_ref, queries_ref),
        semaphore,
    )
    row_count, head_dim = keys_ref.shape
    shard = shard_ref[0]
    assignment = assignment_ref[...]
    weight = row_weight(importance_ref[...])
    target = jnp.where(divided(assignment, row_count) == shard, remainder(assignment, row_count), -1)
    index = lanes_of((1, row_count))
    kept = target == index
    line = rows_of((row_count, row_count))
    mix = jnp.where(target == line, weight, jnp.where((index == line) & jnp.logical_not(kept), 1.0, 0.0)).astype(BF16)
    rows = jnp.concatenate([keys_ref[...], values_ref[...]], axis=1)
    sums_ref[...] = jnp.dot(mix, rows, preferred_element_type=F32)
    total_ref[...] = jnp.dot(mix, jnp.ones((row_count, LANES), BF16), preferred_element_type=F32)
    bias_ref[...] = jnp.broadcast_to(jnp.where(kept, 0.0, -jnp.inf), bias_ref.shape)

    query_rows = queries_ref.shape[0]
    heads = queries_ref.shape[1] // head_dim
    per_peer = query_rows * heads // shards
    span = per_peer + 2
    group = per_peer * heads
    peers = group // per_peer
    peer, place = peer_place(rows_of((peers * span, group)), span)
    per_tile = heads * TILE // per_peer
    head = remainder(peer, per_tile) * (per_peer // TILE) + divided(place, TILE)
    source = head * per_peer + divided(peer, per_tile) * TILE + remainder(place, TILE)
    order = onehot((source == lanes_of((peers * span, group))) & (place < per_peer))
    for part in range(query_rows // per_peer):
        block = queries_ref[part * per_peer : (part + 1) * per_peer, :]
        block = jnp.concatenate([block[:, at * head_dim : (at + 1) * head_dim] for at in range(heads)], axis=0)
        moved = jnp.dot(order, block, preferred_element_type=F32).astype(BF16)
        padded_ref[part * peers * span : (part + 1) * peers * span, :] = moved


def attend_kernel(
    shards, shard_ref, begin_ref, sums_ref, total_ref, bias_ref, padded_ref, far_ref, first_ref, second_ref,
    merged_keys_ref, merged_values_ref, partial_ref,
):
    row_count = sums_ref.shape[0]
    shard = shard_ref[0]
    back = jnp.where(shard == 0, shards - 1, shard - 1)
    ahead = jnp.where(shard == shards - 1, 0, shard + 1)
    is_odd = remainder(shard, 2) == 1
    first = begin_ref[0]
    shard = position(shard, first, shards)
    first_source = position(jnp.where(is_odd, ahead, back), first, shards)
    second_source = position(jnp.where(is_odd, back, ahead), first, shards)

    far = far_ref[...]
    lines = PIECES * shards
    line = rows_of((lines, lines))
    piece = divided(line, shards)
    wanted = remainder(line, shards) * PIECES + piece
    neighbour = jnp.where(line == 3 * shards, first_source, second_source) * PIECES + NOTES
    wanted = jnp.where(piece < 3, wanted, jnp.where(line < 3 * shards + 2, neighbour, -1))
    pieces = jnp.dot(onehot(lanes_of((lines, lines)) == wanted), far, preferred_element_type=F32)
    notes = pieces[2 * shards : 3 * shards]
    if shards < LANES:
        notes = jnp.concatenate([notes, jnp.zeros((LANES - shards, LANES), F32)], axis=0)
    notes = notes.T
    near_notes = pieces[3 * shards : 3 * shards + TILE]
    near_target = (
        pltpu.roll(near_notes, LANES - NEAR, 1) * LANES + pltpu.roll(near_notes, LANES - 2 * NEAR, 1)
    )
    far_target = notes[NEAR : NEAR + 1, :] * LANES + notes[2 * NEAR : 2 * NEAR + 1, :]
    lane = lanes_of((1, LANES))
    near_start = [shards, shards + NEAR]
    is_far = (lane < shards) & (lane != first_source) & (lane != second_source) & (lane != shard)
    target = jnp.where(is_far, far_target, -1.0)
    weight = notes[0:1, :]
    for at, start in enumerate(near_start):
        inside = (lane >= start) & (lane < start + NEAR)
        target = jnp.where(inside, pltpu.roll(near_target, start, 1)[at : at + 1, :], target)
        weight = jnp.where(inside, pltpu.roll(near_notes, start, 1)[at : at + 1, :], weight)
    target = target.astype(jnp.int32)
    mix = jnp.where(target == rows_of((row_count, LANES)), weight, 0.0).astype(BF16)
    unused = jnp.zeros((LANES - shards - 2 * NEAR, 2 * LANES), BF16)
    arrived = jnp.concatenate(
        [jnp.concatenate([pieces[:shards], pieces[shards : 2 * shards]], axis=1).astype(BF16)]
        + [jnp.concatenate([near[:NEAR], near[NEAR:]], axis=1) for near in (first_ref[...], second_ref[...])]
        + [unused],
        axis=0,
    )
    total = total_ref[...] + jnp.dot(mix, jnp.ones((LANES, LANES), BF16), preferred_element_type=F32)
    sums = sums_ref[...] + jnp.dot(mix, arrived, preferred_element_type=F32)
    share = 1.0 / total
    merged_keys = (sums[:, :LANES] * share).astype(BF16)
    merged_values = (sums[:, LANES:] * share).astype(BF16)
    merged_keys_ref[...] = merged_keys
    merged_values_ref[...] = merged_values

    span = padded_ref.shape[0] // shards
    per_peer = span - 2
    bias = bias_ref[0:1, :]
    group = TILE * span
    peer, place = peer_place(rows_of((group, LANES)), span)
    lane = lanes_of((group, LANES))
    diagonal = (place < per_peer) & (lane == peer * per_peer + place)
    inside = place < per_peer
    row = rows_of((TILE, LANES))
    peaks = jnp.zeros((TILE, LANES), F32)
    sizes = jnp.zeros((TILE, LANES), F32)
    starts = range(0, padded_ref.shape[0], group)
    for which, at in enumerate(starts):
        scores = lax.dot_general(
            padded_ref[at : at + group, :], merged_keys, (((1,), (1,)), ((), ())), preferred_element_type=F32
        )
        scores = scores + bias
        peak = jnp.max(scores, axis=1, keepdims=True)
        prob = jnp.exp2((scores - peak) * SCORE_SCALE)
        size = jnp.sum(prob, axis=1, keepdims=True)
        sums = jnp.dot(prob.astype(BF16), merged_values, preferred_element_type=F32)
        peaks = jnp.where(row == which, jnp.sum(jnp.where(diagonal, peak, 0.0), axis=0, keepdims=True), peaks)
        sizes = jnp.where(row == which, jnp.sum(jnp.where(diagonal, size, 0.0), axis=0, keepdims=True), sizes)
        partial_ref[at : at + group, :] = jnp.where(inside, sums, 0.0).astype(BF16)
    part = divided(lanes_of((TILE, LANES)), per_peer)
    members = split_parts(peaks, PEAK_PARTS) + split_parts(sizes, SIZE_PARTS)
    stats = []
    for turn in range(TILE):
        mine = jnp.zeros((TILE, LANES), F32)
        for which, member in enumerate(members):
            shift = (which - turn) * per_peer % LANES
            mine = jnp.where(part == which, pltpu.roll(member, shift, 1) if shift else member, mine)
        stats.append(mine)
    stats = jnp.concatenate(stats, axis=0).astype(BF16)
    peer, place = peer_place(rows_of((group, TILE * TILE)), span)
    source = lanes_of((group, TILE * TILE)) - jnp.where(place == per_peer, peer * TILE, -LANES)
    for which, at in enumerate(starts):
        spread = jnp.dot(onehot(source == which), stats, preferred_element_type=F32)
        partial_ref[at : at + group, :] = (partial_ref[at : at + group, :].astype(F32) + spread).astype(BF16)


def combine_kernel(shards, partial_ref, finished_ref):
    count = partial_ref.shape[0]
    span = count // shards
    per_peer = span - 2
    partial = partial_ref[...]
    wide = (shards, count)
    picked = onehot(lanes_of(wide) == rows_of(wide) * span + per_peer)
    stats = jnp.dot(picked, partial, preferred_element_type=F32)

    def part(which):
        return pltpu.roll(stats, LANES - which * per_peer, 1) if which else stats

    valid = lanes_of((shards, LANES)) < per_peer
    peak = jnp.where(valid, (part(0) + part(1)) + part(2), 0.0)
    size = jnp.where(valid, part(3) + part(4), 1.0)
    rescale = jnp.exp2((peak - jnp.max(peak, axis=0, keepdims=True)) * SCORE_SCALE)
    factor = rescale / jnp.sum(rescale * size, axis=0, keepdims=True)
    factor = jnp.concatenate([factor, jnp.zeros((LANES - shards, LANES), F32)], axis=0).T[:per_peer, :shards]
    factor = jnp.concatenate(split_parts(factor, 2), axis=0).astype(BF16)
    start = rows_of(wide) * span
    spread = onehot((lanes_of(wide) >= start) & (lanes_of(wide) < start + span))
    factor = jnp.dot(factor, spread, preferred_element_type=F32)
    unused, place = peer_place(lanes_of(factor.shape), span)
    factor = jnp.where(place == remainder(rows_of(factor.shape), per_peer), factor, 0.0).astype(BF16)
    total = jnp.dot(factor, partial, preferred_element_type=F32)
    finished = (total[:per_peer] + total[per_peer:]).astype(BF16)
    for peer in range(shards):
        finished_ref[peer] = finished


SMEM = pl.BlockSpec(memory_space=pltpu.SMEM)
VMEM = pl.BlockSpec(memory_space=pltpu.VMEM)
HBM = pl.BlockSpec(memory_space=pltpu.HBM)


def run_kernel(body, shards, shapes, specs, operands, pulled=()):
    scratch = [pltpu.VMEM(member.shape, member.dtype) for member in pulled]
    if pulled:
        scratch.append(pltpu.SemaphoreType.DMA((len(pulled),)))
    return pl.pallas_call(
        functools.partial(body, shards),
        out_shape=[jax.ShapeDtypeStruct(shape, dtype) for shape, dtype in shapes],
        in_specs=specs,
        out_specs=[VMEM] * len(shapes),
        scratch_shapes=scratch,
        compiler_params=pltpu.CompilerParams(vmem_limit_bytes=24 * 1024 * 1024),
    )(*operands)


def per_device(cache_keys, cache_values, importance, assignment, queries):
    row_count, head_dim = cache_keys.shape
    query_rows = queries.shape[0]
    heads = queries.shape[1] // head_dim
    shards = lax.axis_size("ctx")
    groups = lax.axis_size("kv")
    per_peer = query_rows * heads // shards
    span = per_peer + 2
    shard = lax.axis_index("ctx").astype(jnp.int32).reshape(1)
    core = lax.axis_index("kv").astype(jnp.int32) % 2
    begins = [shards * number // 64 for number in ROWS_FIRST]
    begin = (begins[0] + core * (begins[1] - begins[0])).reshape(1)
    assignment = assignment.reshape(1, row_count)

    slices = row_count // LANES
    pulled = (importance,)
    (copies,) = run_kernel(copy_kernel, shards, [((groups * slices, LANES), BF16)], [HBM], pulled, pulled)
    importance = lax.all_to_all(copies.reshape(groups, slices, LANES), "kv", 0, 0, tiled=True)
    pulled = (assignment, cache_keys, cache_values)
    far, first, second, peer = run_kernel(
        rows_kernel,
        shards,
        [
            ((PIECES * shards, LANES), BF16),
            ((2 * NEAR, LANES), BF16),
            ((2 * NEAR, LANES), BF16),
            ((TILE, row_count), jnp.int32),
        ],
        [SMEM, SMEM, HBM, HBM, HBM],
        (shard, begin) + pulled,
        pulled,
    )
    first = lax.ppermute(first, "ctx", [(i, (i - 1 + 2 * (i % 2)) % shards) for i in range(shards)])
    second = lax.ppermute(second, "ctx", [(i, (i + 1 - 2 * (i % 2)) % shards) for i in range(shards)])
    (far,) = run_kernel(
        weigh_kernel, shards, [((PIECES * shards, LANES), BF16)], [VMEM, VMEM, VMEM], (importance, peer, far)
    )
    far, importance = lax.optimization_barrier((far, importance))
    far = exchange(far.reshape(shards, PIECES, LANES), shards, groups, ROWS_FIRST)
    pulled = (assignment, cache_keys, cache_values, queries)
    sums, total, bias, padded = run_kernel(
        home_kernel,
        shards,
        [
            ((row_count, 2 * head_dim), F32),
            ((row_count, LANES), F32),
            ((TILE, row_count), F32),
            ((shards * span, head_dim), BF16),
        ],
        [SMEM, VMEM, HBM, HBM, HBM, HBM],
        (shard, importance) + pulled,
        pulled,
    )
    merged_keys, merged_values, partial = run_kernel(
        attend_kernel,
        shards,
        [(cache_keys.shape, BF16), (cache_keys.shape, BF16), ((shards * span, LANES), BF16)],
        [SMEM] * 2 + [VMEM] * 7,
        (shard, begin, sums, total, bias, padded, far.reshape(shards * PIECES, LANES), first, second),
    )
    partial = exchange(partial.reshape(shards, span // 2, 2, LANES), shards, groups, SUMS_FIRST)
    (finished,) = run_kernel(
        combine_kernel, shards, [((shards, per_peer, LANES), BF16)], [VMEM], (partial.reshape(shards * span, LANES),)
    )
    finished = exchange(finished, shards, groups, SUMS_FIRST)
    tiles = query_rows // TILE
    attended = finished.reshape(tiles, heads, TILE, head_dim).transpose(0, 2, 1, 3)
    return (merged_keys, merged_values, attended.reshape(query_rows, heads * head_dim))


def solution(mesh):
    placed = (P("ctx", "kv"), P("ctx", "kv"), P("kv", "ctx"), P("ctx"), P(None, "kv"))
    return jax.shard_map(
        per_device,
        mesh=mesh,
        in_specs=placed,
        out_specs=(P("ctx", "kv"), P("ctx", "kv"), P(None, "kv")),
        check_vma=False,
    )
```

```python
import functools
import math

import jax
import jax.numpy as jnp
from jax import lax
from jax.experimental import pallas as pl
from jax.experimental.pallas import tpu as pltpu
from jax.sharding import PartitionSpec as P

NEAR = 16
LANES = 128
TILE = 8
PIECES = 4
NOTES = 2
ROWS_FIRST = (11, 47)
SUMS_FIRST = (47, 47)
PEAK_PARTS = 3
SIZE_PARTS = 2
SCORE_SCALE = LANES ** (-0.5) * math.log2(math.e)
F32 = jnp.float32
BF16 = jnp.bfloat16


def exchange(array, shards, groups, firsts):
    members = []
    for group in range(groups):
        first = shards * firsts[group % 2] // 64
        members.append([(first + at) % shards * groups + group for at in range(shards)])
    return lax.all_to_all(array, ("ctx", "kv"), 0, 0, tiled=True, axis_index_groups=members)


def rows_of(shape):
    return lax.broadcasted_iota(jnp.int32, shape, 0)


def lanes_of(shape):
    return lax.broadcasted_iota(jnp.int32, shape, 1)


def onehot(flags):
    return flags.astype(F32).astype(BF16)


def row_weight(importance):
    summed = jnp.sum(importance.astype(F32), axis=0).astype(BF16).astype(F32)
    return jnp.concatenate([summed[at : at + 1, :] for at in range(summed.shape[0])], axis=1)


def split_parts(value, count):
    parts = []
    for _ in range(count):
        rounded = value.astype(BF16).astype(F32)
        parts.append(rounded)
        value = value - rounded
    return parts


def divided(index, size):
    if size & (size - 1):
        return (index * (-(-(1 << 16) // size))) >> 16
    return index >> (size.bit_length() - 1)


def remainder(index, size):
    if size & (size - 1):
        return index - divided(index, size) * size
    return index & (size - 1)


def peer_place(index, span):
    return divided(index, span), remainder(index, span)


def pull(sources, targets, semaphore):
    copies = [
        pltpu.make_async_copy(source, target, semaphore.at[at])
        for at, (source, target) in enumerate(zip(sources, targets))
    ]
    for copy in copies:
        copy.start()
    for copy in copies:
        copy.wait()


def position(shard, first, shards):
    moved = shard - first
    return jnp.where(moved < 0, moved + shards, moved)


def destination(shards, shard, first, assignment, row_count):
    owner = divided(assignment, row_count)
    distance = owner - shard
    distance = jnp.where(distance < 0, distance + shards, distance)
    ahead = distance == 1
    back = distance == shards - 1
    side = rows_of((TILE, row_count))
    flags = jnp.where(side == 0, ahead.astype(F32), jnp.where(side == 1, back.astype(F32), 0.0)).astype(BF16)
    earlier = onehot(rows_of((row_count, row_count)) < lanes_of((row_count, row_count)))
    ranks = jnp.dot(flags, earlier, preferred_element_type=F32).astype(jnp.int32)
    rank = jnp.where(ahead, ranks[0:1, :], jnp.where(back, ranks[1:2, :], 0))
    peer = jnp.where(distance == 0, -1, position(owner, first, shards))
    far_peer = jnp.where(ahead | back, -1, peer)
    return peer, far_peer, ahead, back, rank


def chosen_rows(shards, peer, far_peer, row_count):
    line = rows_of((PIECES * shards, row_count))
    return onehot(divided(line, PIECES) == jnp.where(remainder(line, PIECES) == NOTES, peer, far_peer))


def copy_kernel(shards, importance_hbm, copies_ref, importance_ref, semaphore):
    pull((importance_hbm,), (importance_ref,), semaphore)
    importance = importance_ref[...].astype(F32)
    slices = importance.shape[1] // LANES
    place = remainder(rows_of(copies_ref.shape), slices)
    copies = jnp.zeros(copies_ref.shape, F32)
    for at in range(slices):
        copies = jnp.where(place == at, importance[:, at * LANES : (at + 1) * LANES], copies)
    copies_ref[...] = copies.astype(BF16)


def rows_kernel(
    shards, shard_ref, begin_ref, assignment_hbm, keys_hbm, values_hbm, far_ref, first_ref, second_ref, peer_ref,
    assignment_ref, keys_ref, values_ref, semaphore,
):
    pull((assignment_hbm, keys_hbm, values_hbm), (assignment_ref, keys_ref, values_ref), semaphore)
    row_count = keys_ref.shape[0]
    assignment = assignment_ref[...]
    peer, far_peer, ahead, back, rank = destination(shards, shard_ref[0], begin_ref[0], assignment, row_count)
    rows = jnp.concatenate([keys_ref[...], values_ref[...]], axis=1)
    is_even = 1 - remainder(shard_ref[0], 2)
    slot = jnp.where(ahead, is_even * NEAR + rank, jnp.where(back, (1 - is_even) * NEAR + rank, -1))
    near = jnp.dot(onehot(rows_of((2 * NEAR, row_count)) == slot), rows, preferred_element_type=F32).astype(BF16)
    first_ref[...] = jnp.concatenate([near[:NEAR, :LANES], near[:NEAR, LANES:]], axis=0)
    second_ref[...] = jnp.concatenate([near[NEAR:, :LANES], near[NEAR:, LANES:]], axis=0)
    chosen = chosen_rows(shards, peer, far_peer, row_count)
    picked = jnp.dot(chosen, rows, preferred_element_type=F32)
    target = remainder(assignment, row_count)
    part = rows_of((LANES, row_count))
    place = jnp.where(
        divided(part, NEAR) == 1,
        divided(target, LANES).astype(F32),
        jnp.where(divided(part, NEAR) == 2, remainder(target, LANES).astype(F32), 0.0),
    )
    notes = jnp.where(remainder(part, NEAR) == rank, place, 0.0).astype(BF16)
    noted = lax.dot_general(chosen, notes, (((1,), (1,)), ((), ())), preferred_element_type=F32)
    piece = remainder(rows_of((PIECES * shards, LANES)), PIECES)
    far_ref[...] = jnp.where(
        piece == 0, picked[:, :LANES], jnp.where(piece == 1, picked[:, LANES:], jnp.where(piece == NOTES, noted, 0.0))
    ).astype(BF16)
    at = rows_of((TILE, row_count))
    peer_ref[...] = jnp.where(at == 0, peer, jnp.where(at == 1, far_peer, rank))


def weigh_kernel(shards, importance_ref, peer_ref, far_ref, out_ref):
    row_count = peer_ref.shape[1]
    weight = row_weight(importance_ref[...])
    peer, far_peer, rank = peer_ref[0:1, :], peer_ref[1:2, :], peer_ref[2:3, :]
    chosen = chosen_rows(shards, peer, far_peer, row_count)
    notes = jnp.where(rows_of((LANES, row_count)) == rank, weight, 0.0).astype(BF16)
    noted = lax.dot_general(chosen, notes, (((1,), (1,)), ((), ())), preferred_element_type=F32)
    piece = remainder(rows_of((PIECES * shards, LANES)), PIECES)
    out_ref[...] = (far_ref[...].astype(F32) + jnp.where(piece == NOTES, noted, 0.0)).astype(BF16)


def home_kernel(
    shards, shard_ref, importance_ref, assignment_hbm, keys_hbm, values_hbm, queries_hbm,
    sums_ref, total_ref, bias_ref, padded_ref, kept_rows_ref, assignment_ref, keys_ref, values_ref, queries_ref, semaphore,
):
    pull(
        (assignment_hbm, keys_hbm, values_hbm, queries_hbm),
        (assignment_ref, keys_ref, values_ref, queries_ref),
        semaphore,
    )
    row_count, head_dim = keys_ref.shape
    shard = shard_ref[0]
    assignment = assignment_ref[...]
    weight = row_weight(importance_ref[...])
    target = jnp.where(divided(assignment, row_count) == shard, remainder(assignment, row_count), -1)
    index = lanes_of((1, row_count))
    kept = target == index
    line = rows_of((row_count, row_count))
    mix = jnp.where(target == line, weight, jnp.where((index == line) & jnp.logical_not(kept), 1.0, 0.0)).astype(BF16)
    rows = jnp.concatenate([keys_ref[...], values_ref[...]], axis=1)
    sums_ref[...] = jnp.dot(mix, rows, preferred_element_type=F32)
    total_ref[...] = jnp.dot(mix, jnp.ones((row_count, LANES), BF16), preferred_element_type=F32)
    room = kept_rows_ref.shape[0]
    earlier = onehot(line < lanes_of((row_count, row_count)))
    kept = kept.astype(F32)
    rank = jnp.dot(jnp.broadcast_to(kept, (TILE, row_count)).astype(BF16), earlier, preferred_element_type=F32)[0:1, :]
    rank = jnp.where(kept > 0.0, rank, -1.0).astype(jnp.int32)
    kept_rows_ref[...] = onehot(rows_of((room, row_count)) == rank)
    kept_count = jnp.sum(kept, axis=1, keepdims=True)
    bias_ref[...] = jnp.where(lanes_of(bias_ref.shape).astype(F32) < kept_count, 0.0, -jnp.inf)

    query_rows = queries_ref.shape[0]
    heads = queries_ref.shape[1] // head_dim
    per_peer = query_rows * heads // shards
    span = per_peer + 2
    group = per_peer * heads
    peers = group // per_peer
    peer, place = peer_place(rows_of((peers * span, group)), span)
    per_tile = heads * TILE // per_peer
    head = remainder(peer, per_tile) * (per_peer // TILE) + divided(place, TILE)
    source = head * per_peer + divided(peer, per_tile) * TILE + remainder(place, TILE)
    order = onehot((source == lanes_of((peers * span, group))) & (place < per_peer))
    for part in range(query_rows // per_peer):
        block = queries_ref[part * per_peer : (part + 1) * per_peer, :]
        block = jnp.concatenate([block[:, at * head_dim : (at + 1) * head_dim] for at in range(heads)], axis=0)
        moved = jnp.dot(order, block, preferred_element_type=F32).astype(BF16)
        padded_ref[part * peers * span : (part + 1) * peers * span, :] = moved


def attend_kernel(
    shards, shard_ref, begin_ref, sums_ref, total_ref, bias_ref, padded_ref, kept_rows_ref, far_ref, first_ref, second_ref,
    merged_keys_ref, merged_values_ref, partial_ref,
):
    row_count = sums_ref.shape[0]
    shard = shard_ref[0]
    back = jnp.where(shard == 0, shards - 1, shard - 1)
    ahead = jnp.where(shard == shards - 1, 0, shard + 1)
    is_odd = remainder(shard, 2) == 1
    first = begin_ref[0]
    shard = position(shard, first, shards)
    first_source = position(jnp.where(is_odd, ahead, back), first, shards)
    second_source = position(jnp.where(is_odd, back, ahead), first, shards)

    far = far_ref[...]
    lines = PIECES * shards
    line = rows_of((lines, lines))
    piece = divided(line, shards)
    wanted = remainder(line, shards) * PIECES + piece
    neighbour = jnp.where(line == 3 * shards, first_source, second_source) * PIECES + NOTES
    wanted = jnp.where(piece < 3, wanted, jnp.where(line < 3 * shards + 2, neighbour, -1))
    pieces = jnp.dot(onehot(lanes_of((lines, lines)) == wanted), far, preferred_element_type=F32)
    notes = pieces[2 * shards : 3 * shards]
    if shards < LANES:
        notes = jnp.concatenate([notes, jnp.zeros((LANES - shards, LANES), F32)], axis=0)
    notes = notes.T
    near_notes = pieces[3 * shards : 3 * shards + TILE]
    near_target = (
        pltpu.roll(near_notes, LANES - NEAR, 1) * LANES + pltpu.roll(near_notes, LANES - 2 * NEAR, 1)
    )
    far_target = notes[NEAR : NEAR + 1, :] * LANES + notes[2 * NEAR : 2 * NEAR + 1, :]
    lane = lanes_of((1, LANES))
    near_start = [shards, shards + NEAR]
    is_far = (lane < shards) & (lane != first_source) & (lane != second_source) & (lane != shard)
    target = jnp.where(is_far, far_target, -1.0)
    weight = notes[0:1, :]
    for at, start in enumerate(near_start):
        inside = (lane >= start) & (lane < start + NEAR)
        target = jnp.where(inside, pltpu.roll(near_target, start, 1)[at : at + 1, :], target)
        weight = jnp.where(inside, pltpu.roll(near_notes, start, 1)[at : at + 1, :], weight)
    target = target.astype(jnp.int32)
    mix = jnp.where(target == rows_of((row_count, LANES)), weight, 0.0).astype(BF16)
    unused = jnp.zeros((LANES - shards - 2 * NEAR, 2 * LANES), BF16)
    arrived = jnp.concatenate(
        [jnp.concatenate([pieces[:shards], pieces[shards : 2 * shards]], axis=1).astype(BF16)]
        + [jnp.concatenate([near[:NEAR], near[NEAR:]], axis=1) for near in (first_ref[...], second_ref[...])]
        + [unused],
        axis=0,
    )
    total = total_ref[...] + jnp.dot(mix, jnp.ones((LANES, LANES), BF16), preferred_element_type=F32)
    sums = sums_ref[...] + jnp.dot(mix, arrived, preferred_element_type=F32)
    share = 1.0 / total
    merged_keys = (sums[:, :LANES] * share).astype(BF16)
    merged_values = (sums[:, LANES:] * share).astype(BF16)
    merged_keys_ref[...] = merged_keys
    merged_values_ref[...] = merged_values
    kept = jnp.dot(
        kept_rows_ref[...], jnp.concatenate([merged_keys, merged_values], axis=1), preferred_element_type=F32
    ).astype(BF16)
    kept_keys, kept_values = kept[:, :LANES], kept[:, LANES:]

    span = padded_ref.shape[0] // shards
    per_peer = span - 2
    bias = bias_ref[0:1, :]
    group = TILE * span
    peer, place = peer_place(rows_of((group, LANES)), span)
    lane = lanes_of((group, LANES))
    diagonal = (place < per_peer) & (lane == peer * per_peer + place)
    inside = place < per_peer
    row = rows_of((TILE, LANES))
    peaks = jnp.zeros((TILE, LANES), F32)
    sizes = jnp.zeros((TILE, LANES), F32)
    starts = range(0, padded_ref.shape[0], group)
    for which, at in enumerate(starts):
        scores = lax.dot_general(
            padded_ref[at : at + group, :], kept_keys, (((1,), (1,)), ((), ())), preferred_element_type=F32
        )
        scores = scores + bias
        peak = jnp.max(scores, axis=1, keepdims=True)
        prob = jnp.exp2((scores - peak) * SCORE_SCALE)
        size = jnp.sum(prob, axis=1, keepdims=True)
        sums = jnp.dot(prob.astype(BF16), kept_values, preferred_element_type=F32)
        peaks = jnp.where(row == which, jnp.sum(jnp.where(diagonal, peak, 0.0), axis=0, keepdims=True), peaks)
        sizes = jnp.where(row == which, jnp.sum(jnp.where(diagonal, size, 0.0), axis=0, keepdims=True), sizes)
        partial_ref[at : at + group, :] = jnp.where(inside, sums, 0.0).astype(BF16)
    part = divided(lanes_of((TILE, LANES)), per_peer)
    members = split_parts(peaks, PEAK_PARTS) + split_parts(sizes, SIZE_PARTS)
    stats = []
    for turn in range(TILE):
        mine = jnp.zeros((TILE, LANES), F32)
        for which, member in enumerate(members):
            shift = (which - turn) * per_peer % LANES
            mine = jnp.where(part == which, pltpu.roll(member, shift, 1) if shift else member, mine)
        stats.append(mine)
    stats = jnp.concatenate(stats, axis=0).astype(BF16)
    peer, place = peer_place(rows_of((group, TILE * TILE)), span)
    source = lanes_of((group, TILE * TILE)) - jnp.where(place == per_peer, peer * TILE, -LANES)
    for which, at in enumerate(starts):
        spread = jnp.dot(onehot(source == which), stats, preferred_element_type=F32)
        partial_ref[at : at + group, :] = (partial_ref[at : at + group, :].astype(F32) + spread).astype(BF16)


def combine_kernel(shards, partial_ref, finished_ref):
    count = partial_ref.shape[0]
    span = count // shards
    per_peer = span - 2
    partial = partial_ref[...]
    wide = (shards, count)
    picked = onehot(lanes_of(wide) == rows_of(wide) * span + per_peer)
    stats = jnp.dot(picked, partial, preferred_element_type=F32)

    def part(which):
        return pltpu.roll(stats, LANES - which * per_peer, 1) if which else stats

    valid = lanes_of((shards, LANES)) < per_peer
    peak = jnp.where(valid, (part(0) + part(1)) + part(2), 0.0)
    size = jnp.where(valid, part(3) + part(4), 1.0)
    rescale = jnp.exp2((peak - jnp.max(peak, axis=0, keepdims=True)) * SCORE_SCALE)
    factor = rescale / jnp.sum(rescale * size, axis=0, keepdims=True)
    factor = jnp.concatenate([factor, jnp.zeros((LANES - shards, LANES), F32)], axis=0).T[:per_peer, :shards]
    factor = jnp.concatenate(split_parts(factor, 2), axis=0).astype(BF16)
    start = rows_of(wide) * span
    spread = onehot((lanes_of(wide) >= start) & (lanes_of(wide) < start + span))
    factor = jnp.dot(factor, spread, preferred_element_type=F32)
    unused, place = peer_place(lanes_of(factor.shape), span)
    factor = jnp.where(place == remainder(rows_of(factor.shape), per_peer), factor, 0.0).astype(BF16)
    total = jnp.dot(factor, partial, preferred_element_type=F32)
    finished = (total[:per_peer] + total[per_peer:]).astype(BF16)
    for peer in range(shards):
        finished_ref[peer] = finished


SMEM = pl.BlockSpec(memory_space=pltpu.SMEM)
VMEM = pl.BlockSpec(memory_space=pltpu.VMEM)
HBM = pl.BlockSpec(memory_space=pltpu.HBM)


def run_kernel(body, shards, shapes, specs, operands, pulled=()):
    scratch = [pltpu.VMEM(member.shape, member.dtype) for member in pulled]
    if pulled:
        scratch.append(pltpu.SemaphoreType.DMA((len(pulled),)))
    return pl.pallas_call(
        functools.partial(body, shards),
        out_shape=[jax.ShapeDtypeStruct(shape, dtype) for shape, dtype in shapes],
        in_specs=specs,
        out_specs=[VMEM] * len(shapes),
        scratch_shapes=scratch,
        compiler_params=pltpu.CompilerParams(vmem_limit_bytes=24 * 1024 * 1024),
    )(*operands)


def per_device(cache_keys, cache_values, importance, assignment, queries):
    row_count, head_dim = cache_keys.shape
    query_rows = queries.shape[0]
    heads = queries.shape[1] // head_dim
    shards = lax.axis_size("ctx")
    groups = lax.axis_size("kv")
    per_peer = query_rows * heads // shards
    span = per_peer + 2
    shard = lax.axis_index("ctx").astype(jnp.int32).reshape(1)
    core = lax.axis_index("kv").astype(jnp.int32) % 2
    begins = [shards * number // 64 for number in ROWS_FIRST]
    begin = (begins[0] + core * (begins[1] - begins[0])).reshape(1)
    assignment = assignment.reshape(1, row_count)

    slices = row_count // LANES
    pulled = (importance,)
    (copies,) = run_kernel(copy_kernel, shards, [((groups * slices, LANES), BF16)], [HBM], pulled, pulled)
    importance = lax.all_to_all(copies.reshape(groups, slices, LANES), "kv", 0, 0, tiled=True)
    pulled = (assignment, cache_keys, cache_values)
    far, first, second, peer = run_kernel(
        rows_kernel,
        shards,
        [
            ((PIECES * shards, LANES), BF16),
            ((2 * NEAR, LANES), BF16),
            ((2 * NEAR, LANES), BF16),
            ((TILE, row_count), jnp.int32),
        ],
        [SMEM, SMEM, HBM, HBM, HBM],
        (shard, begin) + pulled,
        pulled,
    )
    first = lax.ppermute(first, "ctx", [(i, (i - 1 + 2 * (i % 2)) % shards) for i in range(shards)])
    second = lax.ppermute(second, "ctx", [(i, (i + 1 - 2 * (i % 2)) % shards) for i in range(shards)])
    (far,) = run_kernel(
        weigh_kernel, shards, [((PIECES * shards, LANES), BF16)], [VMEM, VMEM, VMEM], (importance, peer, far)
    )
    far, importance = lax.optimization_barrier((far, importance))
    far = exchange(far.reshape(shards, PIECES, LANES), shards, groups, ROWS_FIRST)
    pulled = (assignment, cache_keys, cache_values, queries)
    sums, total, bias, padded, kept_rows = run_kernel(
        home_kernel,
        shards,
        [
            ((row_count, 2 * head_dim), F32),
            ((row_count, LANES), F32),
            ((TILE, row_count * 3 // 4), F32),
            ((shards * span, head_dim), BF16),
            ((row_count * 3 // 4, row_count), BF16),
        ],
        [SMEM, VMEM, HBM, HBM, HBM, HBM],
        (shard, importance) + pulled,
        pulled,
    )
    merged_keys, merged_values, partial = run_kernel(
        attend_kernel,
        shards,
        [(cache_keys.shape, BF16), (cache_keys.shape, BF16), ((shards * span, LANES), BF16)],
        [SMEM] * 2 + [VMEM] * 8,
        (shard, begin, sums, total, bias, padded, kept_rows, far.reshape(shards * PIECES, LANES), first, second),
    )
    partial = exchange(partial.reshape(shards, span // 2, 2, LANES), shards, groups, SUMS_FIRST)
    (finished,) = run_kernel(
        combine_kernel, shards, [((shards, per_peer, LANES), BF16)], [VMEM], (partial.reshape(shards * span, LANES),)
    )
    finished = exchange(finished, shards, groups, SUMS_FIRST)
    tiles = query_rows // TILE
    attended = finished.reshape(tiles, heads, TILE, head_dim).transpose(0, 2, 1, 3)
    return (merged_keys, merged_values, attended.reshape(query_rows, heads * head_dim))


def solution(mesh):
    placed = (P("ctx", "kv"), P("ctx", "kv"), P("kv", "ctx"), P("ctx"), P(None, "kv"))
    return jax.shard_map(
        per_device,
        mesh=mesh,
        in_specs=placed,
        out_specs=(P("ctx", "kv"), P("ctx", "kv"), P(None, "kv")),
        check_vma=False,
    )
```

```python
import functools
import math

import jax
import jax.numpy as jnp
from jax import lax
from jax.experimental import pallas as pl
from jax.experimental.pallas import tpu as pltpu
from jax.sharding import PartitionSpec as P

NEAR = 16
LANES = 128
TILE = 8
PIECES = 4
NOTES = 2
ROWS_FIRST = (11, 47)
SUMS_FIRST = (47, 47)
PEAK_PARTS = 3
SIZE_PARTS = 2
SCORE_SCALE = LANES ** (-0.5) * math.log2(math.e)
F32 = jnp.float32
BF16 = jnp.bfloat16


def exchange(array, shards, groups, firsts):
    members = []
    for group in range(groups):
        first = shards * firsts[group % 2] // 64
        members.append([(first + at) % shards * groups + group for at in range(shards)])
    return lax.all_to_all(array, ("ctx", "kv"), 0, 0, tiled=True, axis_index_groups=members)


def rows_of(shape):
    return lax.broadcasted_iota(jnp.int32, shape, 0)


def lanes_of(shape):
    return lax.broadcasted_iota(jnp.int32, shape, 1)


def onehot(flags):
    return flags.astype(F32).astype(BF16)


def row_weight(importance):
    summed = jnp.sum(importance.astype(F32), axis=0).astype(BF16).astype(F32)
    return jnp.concatenate([summed[at : at + 1, :] for at in range(summed.shape[0])], axis=1)


def split_parts(value, count):
    parts = []
    for _ in range(count):
        rounded = value.astype(BF16).astype(F32)
        parts.append(rounded)
        value = value - rounded
    return parts


def divided(index, size):
    if size & (size - 1):
        return (index * (-(-(1 << 16) // size))) >> 16
    return index >> (size.bit_length() - 1)


def remainder(index, size):
    if size & (size - 1):
        return index - divided(index, size) * size
    return index & (size - 1)


def peer_place(index, span):
    return divided(index, span), remainder(index, span)


def pull(sources, targets, semaphore):
    copies = [
        pltpu.make_async_copy(source, target, semaphore.at[at])
        for at, (source, target) in enumerate(zip(sources, targets))
    ]
    for copy in copies:
        copy.start()
    for copy in copies:
        copy.wait()


def position(shard, first, shards):
    moved = shard - first
    return jnp.where(moved < 0, moved + shards, moved)


def destination(shards, shard, first, assignment, row_count):
    owner = divided(assignment, row_count)
    distance = owner - shard
    distance = jnp.where(distance < 0, distance + shards, distance)
    ahead = distance == 1
    back = distance == shards - 1
    side = rows_of((TILE, row_count))
    flags = jnp.where(side == 0, ahead.astype(F32), jnp.where(side == 1, back.astype(F32), 0.0)).astype(BF16)
    earlier = onehot(rows_of((row_count, row_count)) < lanes_of((row_count, row_count)))
    ranks = jnp.dot(flags, earlier, preferred_element_type=F32).astype(jnp.int32)
    rank = jnp.where(ahead, ranks[0:1, :], jnp.where(back, ranks[1:2, :], 0))
    peer = jnp.where(distance == 0, -1, position(owner, first, shards))
    far_peer = jnp.where(ahead | back, -1, peer)
    return peer, far_peer, ahead, back, rank


def chosen_rows(shards, peer, far_peer, row_count):
    line = rows_of((PIECES * shards, row_count))
    return onehot(divided(line, PIECES) == jnp.where(remainder(line, PIECES) == NOTES, peer, far_peer))


def copy_kernel(shards, importance_hbm, copies_ref, importance_ref, semaphore):
    pull((importance_hbm,), (importance_ref,), semaphore)
    importance = importance_ref[...].astype(F32)
    slices = importance.shape[1] // LANES
    place = remainder(rows_of(copies_ref.shape), slices)
    copies = jnp.zeros(copies_ref.shape, F32)
    for at in range(slices):
        copies = jnp.where(place == at, importance[:, at * LANES : (at + 1) * LANES], copies)
    copies_ref[...] = copies.astype(BF16)


def rows_kernel(
    shards, shard_ref, begin_ref, assignment_hbm, keys_hbm, values_hbm, far_ref, first_ref, second_ref, rank_ref, chosen_ref,
    assignment_ref, keys_ref, values_ref, semaphore,
):
    pull((assignment_hbm, keys_hbm, values_hbm), (assignment_ref, keys_ref, values_ref), semaphore)
    row_count = keys_ref.shape[0]
    assignment = assignment_ref[...]
    peer, far_peer, ahead, back, rank = destination(shards, shard_ref[0], begin_ref[0], assignment, row_count)
    rows = jnp.concatenate([keys_ref[...], values_ref[...]], axis=1)
    is_even = 1 - remainder(shard_ref[0], 2)
    slot = jnp.where(ahead, is_even * NEAR + rank, jnp.where(back, (1 - is_even) * NEAR + rank, -1))
    near = jnp.dot(onehot(rows_of((2 * NEAR, row_count)) == slot), rows, preferred_element_type=F32).astype(BF16)
    first_ref[...] = jnp.concatenate([near[:NEAR, :LANES], near[:NEAR, LANES:]], axis=0)
    second_ref[...] = jnp.concatenate([near[NEAR:, :LANES], near[NEAR:, LANES:]], axis=0)
    chosen = chosen_rows(shards, peer, far_peer, row_count)
    picked = jnp.dot(chosen, rows, preferred_element_type=F32)
    target = remainder(assignment, row_count)
    part = rows_of((LANES, row_count))
    place = jnp.where(
        divided(part, NEAR) == 1,
        divided(target, LANES).astype(F32),
        jnp.where(divided(part, NEAR) == 2, remainder(target, LANES).astype(F32), 0.0),
    )
    notes = jnp.where(remainder(part, NEAR) == rank, place, 0.0).astype(BF16)
    noted = lax.dot_general(chosen, notes, (((1,), (1,)), ((), ())), preferred_element_type=F32)
    piece = remainder(rows_of((PIECES * shards, LANES)), PIECES)
    far_ref[...] = jnp.where(
        piece == 0, picked[:, :LANES], jnp.where(piece == 1, picked[:, LANES:], jnp.where(piece == NOTES, noted, 0.0))
    ).astype(BF16)
    rank_ref[...] = jnp.broadcast_to(rank, rank_ref.shape)
    chosen_ref[...] = chosen


def weigh_kernel(shards, importance_ref, rank_ref, chosen_ref, far_ref, out_ref):
    row_count = rank_ref.shape[1]
    weight = row_weight(importance_ref[...])
    notes = jnp.where(rows_of((LANES, row_count)) == rank_ref[0:1, :], weight, 0.0).astype(BF16)
    noted = lax.dot_general(chosen_ref[...], notes, (((1,), (1,)), ((), ())), preferred_element_type=F32)
    piece = remainder(rows_of((PIECES * shards, LANES)), PIECES)
    out_ref[...] = (far_ref[...].astype(F32) + jnp.where(piece == NOTES, noted, 0.0)).astype(BF16)


def home_kernel(
    shards, shard_ref, importance_ref, assignment_hbm, keys_hbm, values_hbm, queries_hbm,
    sums_ref, total_ref, bias_ref, padded_ref, kept_rows_ref, assignment_ref, keys_ref, values_ref, queries_ref, semaphore,
):
    pull(
        (assignment_hbm, keys_hbm, values_hbm, queries_hbm),
        (assignment_ref, keys_ref, values_ref, queries_ref),
        semaphore,
    )
    row_count, head_dim = keys_ref.shape
    shard = shard_ref[0]
    assignment = assignment_ref[...]
    weight = row_weight(importance_ref[...])
    target = jnp.where(divided(assignment, row_count) == shard, remainder(assignment, row_count), -1)
    index = lanes_of((1, row_count))
    kept = target == index
    line = rows_of((row_count, row_count))
    mix = jnp.where(target == line, weight, jnp.where((index == line) & jnp.logical_not(kept), 1.0, 0.0)).astype(BF16)
    rows = jnp.concatenate([keys_ref[...], values_ref[...]], axis=1)
    sums_ref[...] = jnp.dot(mix, rows, preferred_element_type=F32)
    total_ref[...] = jnp.dot(mix, jnp.ones((row_count, LANES), BF16), preferred_element_type=F32)
    room = kept_rows_ref.shape[0]
    earlier = onehot(line < lanes_of((row_count, row_count)))
    kept = kept.astype(F32)
    rank = jnp.dot(jnp.broadcast_to(kept, (TILE, row_count)).astype(BF16), earlier, preferred_element_type=F32)[0:1, :]
    rank = jnp.where(kept > 0.0, rank, -1.0).astype(jnp.int32)
    kept_rows_ref[...] = onehot(rows_of((room, row_count)) == rank)
    kept_count = jnp.sum(kept, axis=1, keepdims=True)
    bias_ref[...] = jnp.where(lanes_of(bias_ref.shape).astype(F32) < kept_count, 0.0, -jnp.inf)

    query_rows = queries_ref.shape[0]
    heads = queries_ref.shape[1] // head_dim
    per_peer = query_rows * heads // shards
    span = per_peer + 2
    group = per_peer * heads
    peers = group // per_peer
    peer, place = peer_place(rows_of((peers * span, group)), span)
    per_tile = heads * TILE // per_peer
    head = remainder(peer, per_tile) * (per_peer // TILE) + divided(place, TILE)
    source = head * per_peer + divided(peer, per_tile) * TILE + remainder(place, TILE)
    order = onehot((source == lanes_of((peers * span, group))) & (place < per_peer))
    for part in range(query_rows // per_peer):
        block = queries_ref[part * per_peer : (part + 1) * per_peer, :]
        block = jnp.concatenate([block[:, at * head_dim : (at + 1) * head_dim] for at in range(heads)], axis=0)
        moved = jnp.dot(order, block, preferred_element_type=F32).astype(BF16)
        padded_ref[part * peers * span : (part + 1) * peers * span, :] = moved


def attend_kernel(
    shards, shard_ref, begin_ref, sums_ref, total_ref, bias_ref, padded_ref, kept_rows_ref, far_ref, first_ref, second_ref,
    merged_keys_ref, merged_values_ref, partial_ref,
):
    row_count = sums_ref.shape[0]
    shard = shard_ref[0]
    back = jnp.where(shard == 0, shards - 1, shard - 1)
    ahead = jnp.where(shard == shards - 1, 0, shard + 1)
    is_odd = remainder(shard, 2) == 1
    first = begin_ref[0]
    shard = position(shard, first, shards)
    first_source = position(jnp.where(is_odd, ahead, back), first, shards)
    second_source = position(jnp.where(is_odd, back, ahead), first, shards)

    far = far_ref[...]
    lines = PIECES * shards
    line = rows_of((lines, lines))
    piece = divided(line, shards)
    wanted = remainder(line, shards) * PIECES + piece
    neighbour = jnp.where(line == 3 * shards, first_source, second_source) * PIECES + NOTES
    wanted = jnp.where(piece < 3, wanted, jnp.where(line < 3 * shards + 2, neighbour, -1))
    pieces = jnp.dot(onehot(lanes_of((lines, lines)) == wanted), far, preferred_element_type=F32)
    notes = pieces[2 * shards : 3 * shards]
    if shards < LANES:
        notes = jnp.concatenate([notes, jnp.zeros((LANES - shards, LANES), F32)], axis=0)
    notes = notes.T
    near_notes = pieces[3 * shards : 3 * shards + TILE]
    near_target = (
        pltpu.roll(near_notes, LANES - NEAR, 1) * LANES + pltpu.roll(near_notes, LANES - 2 * NEAR, 1)
    )
    far_target = notes[NEAR : NEAR + 1, :] * LANES + notes[2 * NEAR : 2 * NEAR + 1, :]
    lane = lanes_of((1, LANES))
    near_start = [shards, shards + NEAR]
    is_far = (lane < shards) & (lane != first_source) & (lane != second_source) & (lane != shard)
    target = jnp.where(is_far, far_target, -1.0)
    weight = notes[0:1, :]
    for at, start in enumerate(near_start):
        inside = (lane >= start) & (lane < start + NEAR)
        target = jnp.where(inside, pltpu.roll(near_target, start, 1)[at : at + 1, :], target)
        weight = jnp.where(inside, pltpu.roll(near_notes, start, 1)[at : at + 1, :], weight)
    target = target.astype(jnp.int32)
    mix = jnp.where(target == rows_of((row_count, LANES)), weight, 0.0).astype(BF16)
    unused = jnp.zeros((LANES - shards - 2 * NEAR, 2 * LANES), BF16)
    arrived = jnp.concatenate(
        [jnp.concatenate([pieces[:shards], pieces[shards : 2 * shards]], axis=1).astype(BF16)]
        + [jnp.concatenate([near[:NEAR], near[NEAR:]], axis=1) for near in (first_ref[...], second_ref[...])]
        + [unused],
        axis=0,
    )
    total = total_ref[...] + jnp.dot(mix, jnp.ones((LANES, LANES), BF16), preferred_element_type=F32)
    sums = sums_ref[...] + jnp.dot(mix, arrived, preferred_element_type=F32)
    share = 1.0 / total
    merged_keys = (sums[:, :LANES] * share).astype(BF16)
    merged_values = (sums[:, LANES:] * share).astype(BF16)
    merged_keys_ref[...] = merged_keys
    merged_values_ref[...] = merged_values
    kept = jnp.dot(
        kept_rows_ref[...], jnp.concatenate([merged_keys, merged_values], axis=1), preferred_element_type=F32
    ).astype(BF16)
    kept_keys, kept_values = kept[:, :LANES], kept[:, LANES:]

    span = padded_ref.shape[0] // shards
    per_peer = span - 2
    bias = bias_ref[0:1, :]
    group = TILE * span
    peer, place = peer_place(rows_of((group, LANES)), span)
    lane = lanes_of((group, LANES))
    diagonal = (place < per_peer) & (lane == peer * per_peer + place)
    inside = place < per_peer
    row = rows_of((TILE, LANES))
    peaks = jnp.zeros((TILE, LANES), F32)
    sizes = jnp.zeros((TILE, LANES), F32)
    starts = range(0, padded_ref.shape[0], group)
    for which, at in enumerate(starts):
        scores = lax.dot_general(
            padded_ref[at : at + group, :], kept_keys, (((1,), (1,)), ((), ())), preferred_element_type=F32
        )
        scores = scores + bias
        peak = jnp.max(scores, axis=1, keepdims=True)
        prob = jnp.exp2((scores - peak) * SCORE_SCALE)
        size = jnp.sum(prob, axis=1, keepdims=True)
        sums = jnp.dot(prob.astype(BF16), kept_values, preferred_element_type=F32)
        peaks = jnp.where(row == which, jnp.sum(jnp.where(diagonal, peak, 0.0), axis=0, keepdims=True), peaks)
        sizes = jnp.where(row == which, jnp.sum(jnp.where(diagonal, size, 0.0), axis=0, keepdims=True), sizes)
        partial_ref[at : at + group, :] = jnp.where(inside, sums, 0.0).astype(BF16)
    part = divided(lanes_of((TILE, LANES)), per_peer)
    members = split_parts(peaks, PEAK_PARTS) + split_parts(sizes, SIZE_PARTS)
    stats = []
    for turn in range(TILE):
        mine = jnp.zeros((TILE, LANES), F32)
        for which, member in enumerate(members):
            shift = (which - turn) * per_peer % LANES
            mine = jnp.where(part == which, pltpu.roll(member, shift, 1) if shift else member, mine)
        stats.append(mine)
    stats = jnp.concatenate(stats, axis=0).astype(BF16)
    peer, place = peer_place(rows_of((group, TILE * TILE)), span)
    source = lanes_of((group, TILE * TILE)) - jnp.where(place == per_peer, peer * TILE, -LANES)
    for which, at in enumerate(starts):
        spread = jnp.dot(onehot(source == which), stats, preferred_element_type=F32)
        partial_ref[at : at + group, :] = (partial_ref[at : at + group, :].astype(F32) + spread).astype(BF16)


def combine_kernel(shards, partial_ref, finished_ref):
    count = partial_ref.shape[0]
    span = count // shards
    per_peer = span - 2
    partial = partial_ref[...]
    wide = (shards, count)
    picked = onehot(lanes_of(wide) == rows_of(wide) * span + per_peer)
    stats = jnp.dot(picked, partial, preferred_element_type=F32)

    def part(which):
        return pltpu.roll(stats, LANES - which * per_peer, 1) if which else stats

    valid = lanes_of((shards, LANES)) < per_peer
    peak = jnp.where(valid, (part(0) + part(1)) + part(2), 0.0)
    size = jnp.where(valid, part(3) + part(4), 1.0)
    rescale = jnp.exp2((peak - jnp.max(peak, axis=0, keepdims=True)) * SCORE_SCALE)
    factor = rescale / jnp.sum(rescale * size, axis=0, keepdims=True)
    factor = jnp.concatenate([factor, jnp.zeros((LANES - shards, LANES), F32)], axis=0).T[:per_peer, :shards]
    factor = jnp.concatenate(split_parts(factor, 2), axis=0).astype(BF16)
    start = rows_of(wide) * span
    spread = onehot((lanes_of(wide) >= start) & (lanes_of(wide) < start + span))
    factor = jnp.dot(factor, spread, preferred_element_type=F32)
    unused, place = peer_place(lanes_of(factor.shape), span)
    factor = jnp.where(place == remainder(rows_of(factor.shape), per_peer), factor, 0.0).astype(BF16)
    total = jnp.dot(factor, partial, preferred_element_type=F32)
    finished = (total[:per_peer] + total[per_peer:]).astype(BF16)
    for peer in range(shards):
        finished_ref[peer] = finished


SMEM = pl.BlockSpec(memory_space=pltpu.SMEM)
VMEM = pl.BlockSpec(memory_space=pltpu.VMEM)
HBM = pl.BlockSpec(memory_space=pltpu.HBM)


def run_kernel(body, shards, shapes, specs, operands, pulled=()):
    scratch = [pltpu.VMEM(member.shape, member.dtype) for member in pulled]
    if pulled:
        scratch.append(pltpu.SemaphoreType.DMA((len(pulled),)))
    return pl.pallas_call(
        functools.partial(body, shards),
        out_shape=[jax.ShapeDtypeStruct(shape, dtype) for shape, dtype in shapes],
        in_specs=specs,
        out_specs=[VMEM] * len(shapes),
        scratch_shapes=scratch,
        compiler_params=pltpu.CompilerParams(vmem_limit_bytes=24 * 1024 * 1024),
    )(*operands)


def per_device(cache_keys, cache_values, importance, assignment, queries):
    row_count, head_dim = cache_keys.shape
    query_rows = queries.shape[0]
    heads = queries.shape[1] // head_dim
    shards = lax.axis_size("ctx")
    groups = lax.axis_size("kv")
    per_peer = query_rows * heads // shards
    span = per_peer + 2
    shard = lax.axis_index("ctx").astype(jnp.int32).reshape(1)
    core = lax.axis_index("kv").astype(jnp.int32) % 2
    begins = [shards * number // 64 for number in ROWS_FIRST]
    begin = (begins[0] + core * (begins[1] - begins[0])).reshape(1)
    assignment = assignment.reshape(1, row_count)

    slices = row_count // LANES
    pulled = (importance,)
    (copies,) = run_kernel(copy_kernel, shards, [((groups * slices, LANES), BF16)], [HBM], pulled, pulled)
    importance = lax.all_to_all(copies.reshape(groups, slices, LANES), "kv", 0, 0, tiled=True)
    pulled = (assignment, cache_keys, cache_values)
    far, first, second, rank, chosen = run_kernel(
        rows_kernel,
        shards,
        [
            ((PIECES * shards, LANES), BF16),
            ((2 * NEAR, LANES), BF16),
            ((2 * NEAR, LANES), BF16),
            ((TILE, row_count), jnp.int32),
            ((PIECES * shards, row_count), BF16),
        ],
        [SMEM, SMEM, HBM, HBM, HBM],
        (shard, begin) + pulled,
        pulled,
    )
    first = lax.ppermute(first, "ctx", [(i, (i - 1 + 2 * (i % 2)) % shards) for i in range(shards)])
    second = lax.ppermute(second, "ctx", [(i, (i + 1 - 2 * (i % 2)) % shards) for i in range(shards)])
    (far,) = run_kernel(
        weigh_kernel, shards, [((PIECES * shards, LANES), BF16)], [VMEM] * 4, (importance, rank, chosen, far)
    )
    far, importance = lax.optimization_barrier((far, importance))
    far = exchange(far.reshape(shards, PIECES, LANES), shards, groups, ROWS_FIRST)
    pulled = (assignment, cache_keys, cache_values, queries)
    sums, total, bias, padded, kept_rows = run_kernel(
        home_kernel,
        shards,
        [
            ((row_count, 2 * head_dim), F32),
            ((row_count, LANES), F32),
            ((TILE, row_count * 3 // 4), F32),
            ((shards * span, head_dim), BF16),
            ((row_count * 3 // 4, row_count), BF16),
        ],
        [SMEM, VMEM, HBM, HBM, HBM, HBM],
        (shard, importance) + pulled,
        pulled,
    )
    merged_keys, merged_values, partial = run_kernel(
        attend_kernel,
        shards,
        [(cache_keys.shape, BF16), (cache_keys.shape, BF16), ((shards * span, LANES), BF16)],
        [SMEM] * 2 + [VMEM] * 8,
        (shard, begin, sums, total, bias, padded, kept_rows, far.reshape(shards * PIECES, LANES), first, second),
    )
    partial = exchange(partial.reshape(shards, span // 2, 2, LANES), shards, groups, SUMS_FIRST)
    (finished,) = run_kernel(
        combine_kernel, shards, [((shards, per_peer, LANES), BF16)], [VMEM], (partial.reshape(shards * span, LANES),)
    )
    finished = exchange(finished, shards, groups, SUMS_FIRST)
    tiles = query_rows // TILE
    attended = finished.reshape(tiles, heads, TILE, head_dim).transpose(0, 2, 1, 3)
    return (merged_keys, merged_values, attended.reshape(query_rows, heads * head_dim))


def solution(mesh):
    placed = (P("ctx", "kv"), P("ctx", "kv"), P("kv", "ctx"), P("ctx"), P(None, "kv"))
    return jax.shard_map(
        per_device,
        mesh=mesh,
        in_specs=placed,
        out_specs=(P("ctx", "kv"), P("ctx", "kv"), P(None, "kv")),
        check_vma=False,
    )
```
